32 devices in a mesh: seq: 4 (over y, x), fsdp: 8 (over z, core).
Axes of the slice: x: 2, y: 2, z: 4, core: 2. Of those that a mesh axis runs over, the one named last changes fastest.
Arguments:
- inputs: bfloat16 [8, 1024, 2048], P('fsdp', 'seq'), may hold values from -6 to 6
- doc_starts: int32 [8, 8], P('fsdp'), may hold values from 0 to 1023, as said below
- ln_gain: bfloat16 [2048], P('fsdp'), may hold values from 0.5 to 1.5
- ln_bias: bfloat16 [2048], P('fsdp'), may hold values from -0.5 to 0.5
- w_qkv: bfloat16 [2048, 6144], P('fsdp'), may hold values from -0.125 to 0.125
- b_qkv: bfloat16 [6144], P('fsdp'), may hold values from -0.5 to 0.5
- w_out: bfloat16 [2048, 2048], P('fsdp'), may hold values from -0.75 to 0.75
- b_out: bfloat16 [2048], P('fsdp'), may hold values from -0.5 to 0.5
- w_fc1: bfloat16 [2048, 8192], P('fsdp'), may hold values from -0.125 to 0.125
- b_fc1: bfloat16 [8192], P('fsdp'), may hold values from -0.5 to 0.5
- w_fc2: bfloat16 [8192, 2048], P('fsdp'), may hold values from -0.0625 to 0.0625
- b_fc2: bfloat16 [2048], P('fsdp'), may hold values from -0.5 to 0.5
- cotangent: bfloat16 [8, 1024, 2048], P('fsdp', 'seq'), may hold values from -6 to 6
Outputs:
- output: bfloat16 [8, 1024, 2048], P('fsdp', 'seq')
- grad_inputs: float32 [8, 1024, 2048], P('fsdp', 'seq')
- grad_ln_gain: float32 [2048], P('fsdp')
- grad_ln_bias: float32 [2048], P('fsdp')
- grad_w_qkv: float32 [2048, 6144], P('fsdp')
- grad_b_qkv: float32 [6144], P('fsdp')
- grad_w_out: float32 [2048, 2048], P('fsdp')
- grad_b_out: float32 [2048], P('fsdp')
- grad_w_fc1: float32 [2048, 8192], P('fsdp')
- grad_b_fc1: float32 [8192], P('fsdp')
- grad_w_fc2: float32 [8192, 2048], P('fsdp')
- grad_b_fc2: float32 [2048], P('fsdp')
The draws below stay inside these ranges and needn't reach their ends.
Inputs may be any that keep to these rules, and one draw needn't show every extreme that they name: `doc_starts`: in every sequence the starts rise strictly, the first is 0 and the last is 1023; document k covers the positions from its start up to the next start, the last one only position 1023.
All inputs are finite; a program needn't handle non-finite values.
Results may differ from the reference program's by a relative error of at most 0.009.
Values may be sent and summed in bfloat16 or wider, within the bound.
No kernel may reach another device: no remote copies, remote signals or barrier semaphores. Data moves between devices by JAX's collectives and lax.ppermute only.
A program may use at most 704 MiB of HBM per device.

```python
from functools import partial
import jax
import jax.numpy as jnp
from jax import lax

D = 2048
HEADS = 32
HEAD_DIM = 64
FF = 8192
ROT = 32
NDOC = 8
SEQ_LEN = 1024
SEQS = 8


def draw_doc_starts(key, part):
    keys = jax.random.split(key, SEQS)

    def one_sequence(seq_key):
        picked = jax.random.permutation(seq_key, SEQ_LEN - 2)[:NDOC - 2] + 1
        first = jnp.zeros((1,), jnp.int32)
        final = jnp.full((1,), SEQ_LEN - 1, jnp.int32)
        return jnp.concatenate([first, jnp.sort(picked).astype(jnp.int32), final])
    return jax.vmap(one_sequence)(keys)


def steps_of(rng, shape, pieces, least, top_value):
    level, own = 1.0, jax.random.fold_in(rng, 6)
    for axis_at, shards_of in pieces:
        draws = jnp.exp(jax.random.uniform(jax.random.fold_in(own, axis_at), (shards_of,), jnp.float32, least / len(pieces), top_value / len(pieces)))
        level = level * jnp.repeat(draws, shape[axis_at] // shards_of).reshape([-1 if axis == axis_at else 1 for axis in range(len(shape))])
    return level


def scatter_about(own_key, dims, spread, reach, cuts=(), held_as=jnp.bfloat16):
    values = jax.random.normal(own_key, dims, jnp.float32) * spread
    if len(cuts) > 0:
        values = steps_of(own_key, dims, cuts, -0.22, 0.18) * values
    return jnp.clip(values, min=-reach, max=reach).astype(held_as)


def setup_inputs(seed: int = 0) -> dict:
    splits = jax.random.split(jax.random.key(seed), 14)
    inputs = scatter_about(splits[0], (SEQS, SEQ_LEN, D), 1.0, 6.0, ((0, 8), (1, 4)))
    doc_starts = draw_doc_starts(jax.random.fold_in(splits[13], 71), 0)
    ln_gain = jnp.clip(1.0 + 0.1 * jax.random.normal(splits[2], (D,), jnp.float32), 0.5, 1.5).astype(jnp.bfloat16)
    ln_bias = scatter_about(splits[3], (D,), 0.1, 0.5, ((0, 8),))
    w_qkv = scatter_about(splits[4], (D, 3 * D), D ** -0.5, 0.125, ((0, 8),))
    b_qkv = scatter_about(splits[5], (3 * D,), 0.1, 0.5, ((0, 8),))
    w_out = scatter_about(splits[6], (D, D), (D // 32) ** -0.5, 0.75, ((0, 8),))
    b_out = scatter_about(splits[7], (D,), 0.1, 0.5, ((0, 8),))
    w_fc1 = scatter_about(splits[8], (D, FF), D ** -0.5, 0.125, ((0, 8),))
    b_fc1 = scatter_about(splits[9], (FF,), 0.1, 0.5, ((0, 8),))
    w_fc2 = scatter_about(splits[10], (FF, D), FF ** -0.5, 0.0625, ((0, 8),))
    b_fc2 = scatter_about(splits[11], (D,), 0.1, 0.5, ((0, 8),))
    cotangent = scatter_about(splits[12], (SEQS, SEQ_LEN, D), 1.0, 6.0, ((0, 8), (1, 4)))
    return {"inputs": inputs, "doc_starts": doc_starts, "ln_gain": ln_gain, "ln_bias": ln_bias, "w_qkv": w_qkv, "b_qkv": b_qkv, "w_out": w_out, "b_out": b_out, "w_fc1": w_fc1, "b_fc1": b_fc1, "w_fc2": w_fc2, "b_fc2": b_fc2, "cotangent": cotangent}


@jax.custom_vjp
def low(v):
    return lax.optimization_barrier(v.astype(jnp.bfloat16)).astype(jnp.float32)

@jax.custom_vjp
def low_back(v):
    return v

def low_keep(v):
    return (low(v), None)

def low_pass(kept, grad):
    return (grad,)

def back_keep(v):
    return (v, None)

def back_low(kept, grad):
    return (low(grad),)
low.defvjp(low_keep, low_pass)
low_back.defvjp(back_keep, back_low)
exact_mode = lax.Precision.HIGHEST
eps_norm = 1e-05

def gelu_tanh(values):
    return 0.5 * values * (1.0 + jnp.tanh(0.7978845608028654 * (values + 0.044715 * values * values * values)))

def rotate(pairs, cosine, sine):
    half_rot = cosine.shape[-1]
    leading = pairs[..., :half_rot]
    trailing = pairs[..., half_rot:2 * half_rot]
    return jnp.concatenate([leading * cosine - trailing * sine, trailing * cosine + leading * sine, pairs[..., 2 * half_rot:]], axis=-1)

def segments(starts_row, positions):
    before = starts_row[None, :] <= positions[:, None]
    opening = lax.optimization_barrier(jnp.max(jnp.where(before, starts_row[None, :], 0), axis=1))
    return (opening, lax.optimization_barrier(jnp.sum(before.astype(jnp.int32), axis=1)))

def turning(starts_row, positions):
    opening, unused = segments(starts_row, positions)
    rates = 10000.0 ** (-2.0 * jnp.arange(ROT // 2, dtype=jnp.float32) / ROT)
    angle = (positions - opening).astype(jnp.float32)[:, None] * rates[None, :]
    return (jnp.cos(angle), jnp.sin(angle))

def attend(packed, segment, positions):
    length = packed.shape[0]
    block_rows = min(512, length)
    query_all = packed[:, :, 0]
    key_all = packed[:, :, 1]
    value_all = packed[:, :, 2]
    score_scale = HEAD_DIM ** (-0.5)

    def one_block(index):
        begin = index * block_rows
        query_rows = lax.dynamic_slice_in_dim(query_all, begin, block_rows, 0)
        query_pos = lax.dynamic_slice_in_dim(positions, begin, block_rows, 0)
        query_seg = lax.dynamic_slice_in_dim(segment, begin, block_rows, 0)
        raw = jnp.einsum('qhd,khd->hqk', query_rows, key_all, precision=exact_mode) * score_scale
        allowed = (positions[None, :] <= query_pos[:, None]) & (segment[None, :] == query_seg[:, None])
        scores = low_back(jnp.where(allowed[None], raw, -1000000000.0))
        top_score = lax.optimization_barrier(jnp.max(scores, axis=-1, keepdims=True))
        expo = jnp.exp(scores - top_score)
        probs = low(expo / lax.optimization_barrier(jnp.sum(expo, axis=-1, keepdims=True)))
        return jnp.einsum('hqk,khd->qhd', probs, value_all, precision=exact_mode)
    mixed = lax.map(jax.checkpoint(one_block), jnp.arange(length // block_rows, dtype=jnp.int32))
    return mixed.reshape(length, HEADS * HEAD_DIM)

def forward(starts_row, rows_in, gain, shift, w_qkv, b_qkv, w_out, b_out, w_fc1, b_fc1, w_fc2, b_fc2):
    length = rows_in.shape[0]
    centred = rows_in - lax.optimization_barrier(jnp.mean(rows_in, axis=-1, keepdims=True))
    inv_std = lax.rsqrt(lax.optimization_barrier(jnp.mean(centred * centred, axis=-1, keepdims=True)) + eps_norm)
    normed = low(centred * inv_std * gain + shift)
    projected = low_back(jnp.dot(normed, w_qkv, precision=exact_mode) + b_qkv)
    projected = projected.reshape(length, HEADS, 3, HEAD_DIM)
    positions = jnp.arange(length, dtype=jnp.int32)
    cosine, sine = turning(starts_row, positions)
    unused_open, segment = segments(starts_row, positions)
    turned = rotate(projected[:, :, :2], cosine[:, None, None, :], sine[:, None, None, :])
    packed = low(low_back(jnp.concatenate([turned, projected[:, :, 2:]], axis=2)))
    mixed = low(low_back(attend(packed, segment, positions)))
    attn_out = jnp.dot(mixed, w_out, precision=exact_mode) + b_out
    hidden = low_back(jnp.dot(normed, w_fc1, precision=exact_mode) + b_fc1)
    active = low(gelu_tanh(hidden))
    return rows_in + attn_out + jnp.dot(active, w_fc2, precision=exact_mode) + b_fc2

def reference(inputs, doc_starts, ln_gain, ln_bias, w_qkv, b_qkv, w_out, b_out, w_fc1, b_fc1, w_fc2, b_fc2, cotangent):
    params = tuple((weight.astype(jnp.float32) for weight in (ln_gain, ln_bias, w_qkv, b_qkv, w_out, b_out, w_fc1, b_fc1, w_fc2, b_fc2)))

    def one_sequence(running, item):
        rows_in, starts_row, grad_rows = item
        result, pullback = jax.vjp(partial(forward, starts_row), rows_in.astype(jnp.float32), *params)
        grads = pullback(grad_rows.astype(jnp.float32))
        running = tuple((total + grad for total, grad in zip(running, grads[1:])))
        return (running, (result.astype(jnp.bfloat16), grads[0]))
    zeros = tuple((jnp.zeros(weight.shape, jnp.float32) for weight in params))
    totals, (output, grad_inputs) = lax.scan(one_sequence, zeros, (inputs, doc_starts, cotangent))
    return (output, grad_inputs, totals[0], totals[1], totals[2], totals[3], totals[4], totals[5], totals[6], totals[7], totals[8], totals[9])
```

```python
import jax
import jax.numpy as jnp
from jax import lax
from jax.sharding import PartitionSpec as P

HEADS = 32
HEAD_DIM = 64
ROT = 32
EPS = 1e-05
BF = jnp.bfloat16
F32 = jnp.float32


def gelu_tanh(values):
    return (
        0.5
        * values
        * (1.0 + jnp.tanh(0.7978845608028654 * (values + 0.044715 * values * values * values)))
    )


def segments(starts_row, positions):
    before = starts_row[None, :] <= positions[:, None]
    opening = jnp.max(jnp.where(before, starts_row[None, :], 0), axis=1)
    return (opening, jnp.sum(before.astype(jnp.int32), axis=1))


def turning(starts_row, positions):
    opening, unused = segments(starts_row, positions)
    rates = 10000.0 ** (-2.0 * jnp.arange(ROT // 2, dtype=F32) / ROT)
    angle = (positions - opening).astype(F32)[:, None] * rates[None, :]
    return (jnp.cos(angle), jnp.sin(angle))


def rotate(pairs, cosine, sine):
    half = cosine.shape[-1]
    lead, trail = pairs[..., :half], pairs[..., half : 2 * half]
    return jnp.concatenate(
        [lead * cosine - trail * sine, trail * cosine + lead * sine, pairs[..., 2 * half :]],
        axis=-1,
    )


def mm(left, right, left_dim=1, right_dim=0):
    return lax.dot_general(
        left, right, (((left_dim,), (right_dim,)), ((), ())), preferred_element_type=F32
    )


def pick(array, index, axis=0):
    return lax.dynamic_index_in_dim(array, index, axis, keepdims=False)


def swap_seq(array, step):
    count = lax.axis_size("seq")
    return lax.ppermute(array, "seq", [(i, i ^ step) for i in range(count)])


def seq_gather(block):
    count = lax.axis_size("seq")
    me = lax.axis_index("seq")
    whole = jnp.zeros((count,) + block.shape, block.dtype)
    whole = lax.dynamic_update_index_in_dim(whole, block, me, 0)
    for step in range(1, count):
        whole = lax.dynamic_update_index_in_dim(whole, swap_seq(block, step), me ^ step, 0)
    return whole


def seq_sum(blocks):
    count = lax.axis_size("seq")
    me = lax.axis_index("seq")
    total = pick(blocks, me).astype(F32)
    for step in range(1, count):
        total = total + swap_seq(pick(blocks, me ^ step), step).astype(F32)
    return total


def line_sum(parts):
    count = parts.shape[0]
    chips = count // 2
    me = lax.axis_index("fsdp")
    chip, core = me // 2, me % 2
    parts = parts.reshape((chips, 2) + parts.shape[1:])
    got = lax.ppermute(pick(parts, 1 - core, 1), "fsdp", [(i, i ^ 1) for i in range(count)])
    own = (pick(parts, core, 1).astype(F32) + got.astype(F32)).astype(parts.dtype)

    def of(index):
        return pick(own, jnp.clip(index, 0, chips - 1))

    total = of(chip).astype(F32)
    down, up = of(chip - (chips - 1)), of(chip + (chips - 1))
    for step in range(1, chips):
        down_pairs = [(2 * a + c, 2 * (a - 1) + c) for a in range(chips - step, chips) for c in (0, 1)]
        up_pairs = [(2 * a + c, 2 * (a + 1) + c) for a in range(0, step) for c in (0, 1)]
        got_down = lax.ppermute(down, "fsdp", down_pairs).astype(F32)
        got_up = lax.ppermute(up, "fsdp", up_pairs).astype(F32)
        if step < chips - 1:
            down = (got_down + of(chip - (chips - step - 1)).astype(F32)).astype(parts.dtype)
            up = (got_up + of(chip + (chips - step - 1)).astype(F32)).astype(parts.dtype)
    return total + got_down + got_up


def fsdp_gather(block):
    return lax.all_gather(block, "fsdp", axis=0, tiled=True)


def attention(query, key, value, grad_of, seg, score_scale):
    length = query.shape[0]
    rows = min(512, length)
    blocks = length // rows
    pos = jnp.arange(length, dtype=jnp.int32)

    def block_scores(index):
        begin = index * rows
        raw = (
            jnp.einsum(
                "qhd,khd->hqk",
                lax.dynamic_slice_in_dim(query, begin, rows, 0),
                key,
                preferred_element_type=F32,
            )
            * score_scale
        )
        q_pos = lax.dynamic_slice_in_dim(pos, begin, rows, 0)
        q_seg = lax.dynamic_slice_in_dim(seg, begin, rows, 0)
        allowed = (pos[None, :] <= q_pos[:, None]) & (seg[None, :] == q_seg[:, None])
        return jnp.where(allowed[None], raw, -1000000000.0)

    def forward_block(index):
        scores = block_scores(index)
        top = jnp.max(scores, axis=-1, keepdims=True)
        expo = jnp.exp(scores - top)
        totals = jnp.sum(expo, axis=-1, keepdims=True)
        probs = (expo / totals).astype(BF)
        return (
            jnp.einsum("hqk,khd->qhd", probs, value, preferred_element_type=F32),
            top + jnp.log(totals),
        )

    mixed, log_norms = lax.map(forward_block, jnp.arange(blocks, dtype=jnp.int32))
    mixed = mixed.reshape(query.shape).astype(BF)
    grad_heads = grad_of()

    def backward_block(carry, item):
        grad_key, grad_value = carry
        index, log_norm = item
        begin = index * rows
        q_rows = lax.dynamic_slice_in_dim(query, begin, rows, 0)
        g_rows = lax.dynamic_slice_in_dim(grad_heads, begin, rows, 0)
        probs = jnp.exp(block_scores(index) - log_norm)
        grad_probs = jnp.einsum("qhd,khd->hqk", g_rows, value, preferred_element_type=F32)
        dots = jnp.sum(probs * grad_probs, axis=-1, keepdims=True)
        grad_scores = (probs * (grad_probs - dots)).astype(BF)
        grad_query = (
            jnp.einsum("hqk,khd->qhd", grad_scores, key, preferred_element_type=F32) * score_scale
        )
        grad_key = (
            grad_key
            + jnp.einsum("hqk,qhd->khd", grad_scores, q_rows, preferred_element_type=F32)
            * score_scale
        )
        grad_value = grad_value + jnp.einsum(
            "hqk,qhd->khd", probs.astype(BF), g_rows, preferred_element_type=F32
        )
        return ((grad_key, grad_value), grad_query)

    zero = jnp.zeros(query.shape, F32)
    (grad_key, grad_value), grad_query = lax.scan(
        backward_block, (zero, zero), (jnp.arange(blocks, dtype=jnp.int32), log_norms)
    )
    return mixed, grad_query.reshape(query.shape), grad_key, grad_value


def per_device(
    inputs,
    doc_starts,
    ln_gain,
    ln_bias,
    w_qkv,
    b_qkv,
    w_out,
    b_out,
    w_fc1,
    b_fc1,
    w_fc2,
    b_fc2,
    cotangent,
):
    seqs = lax.axis_size("seq")
    shards = lax.axis_size("fsdp")
    me = lax.axis_index("seq")
    tok, width = inputs.shape[1:]
    length = tok * seqs
    rows_here = w_qkv.shape[0]
    heads = HEADS // seqs
    head_cols = heads * HEAD_DIM
    shard_heads = w_out.shape[0] // HEAD_DIM
    strided = shard_heads % seqs == 0
    unit = w_fc2.shape[0] // seqs
    hidden_cols = unit * shards
    score_scale = HEAD_DIM ** (-0.5)

    fc1_here = pick(w_fc1.reshape(rows_here, shards, seqs, unit), me, 2).reshape(
        rows_here, hidden_cols
    )
    fc2_here = pick(w_fc2.reshape(seqs, unit, width), me)
    if strided:
        each = shard_heads // seqs
        qkv_here = pick(w_qkv.reshape(rows_here, shards, seqs, each, 3, HEAD_DIM), me, 2)
        out_here = pick(w_out.reshape(seqs, each * HEAD_DIM, width), me)
    else:
        qkv_here = pick(w_qkv.reshape(rows_here, seqs, heads, 3, HEAD_DIM), me, 1)
        out_here = w_out
    qkv_here = qkv_here.reshape(rows_here, heads, 3, HEAD_DIM).transpose(0, 2, 1, 3)
    qkv_here = qkv_here.reshape(rows_here, 3 * head_cols)

    fc1 = fsdp_gather(fc1_here)
    fc2 = fsdp_gather(fc2_here)
    qkv_w = fsdp_gather(qkv_here)
    out_w = fsdp_gather(out_here)
    if not strided:
        out_w = pick(out_w.reshape(seqs, head_cols, width), me)

    sizes = [v.shape[0] for v in (ln_gain, ln_bias, b_out, b_fc2, b_qkv, b_fc1)]
    small = fsdp_gather(jnp.concatenate([ln_gain, ln_bias, b_out, b_fc2, b_qkv, b_fc1])[None])
    small = small.astype(F32)
    cuts = [sum(sizes[:i]) for i in range(len(sizes) + 1)]
    gain, shift, bias_out, bias_fc2, bias_qkv, bias_fc1 = [
        small[:, a:b].reshape(-1) for a, b in zip(cuts[:-1], cuts[1:])
    ]
    bias_fc1 = pick(bias_fc1.reshape(shards, seqs, unit), me, 1).reshape(hidden_cols)
    if strided:
        bias_qkv = pick(bias_qkv.reshape(shards, seqs, each, 3, HEAD_DIM), me, 1)
    else:
        bias_qkv = pick(bias_qkv.reshape(seqs, heads, 3, HEAD_DIM), me)
    bias_qkv = bias_qkv.reshape(heads, 3, HEAD_DIM).transpose(1, 0, 2).reshape(3 * head_cols)

    rows_all = seq_gather(inputs[0]).reshape(length, width)
    grad_rows = seq_gather(cotangent[0]).reshape(length, width)
    starts_row = doc_starts[0]
    pos = jnp.arange(length, dtype=jnp.int32)
    unused_open, seg = segments(starts_row, pos)
    cosine, sine = turning(starts_row, pos)
    cosine, sine = cosine[:, None, :], sine[:, None, :]

    centred = rows_all.astype(F32)
    centred = centred - jnp.mean(centred, axis=-1, keepdims=True)
    inv_std = lax.rsqrt(jnp.mean(centred * centred, axis=-1, keepdims=True) + EPS)
    normal_hat = centred * inv_std
    normed = (normal_hat * gain + shift).astype(BF)

    hidden = mm(normed, fc1) + bias_fc1
    active, pull = jax.vjp(gelu_tanh, hidden)
    active = active.astype(BF)
    part_fc2 = line_sum(mm(active, grad_rows, 0, 0).astype(BF).reshape(shards, unit, width))
    grad_hidden = pull(mm(grad_rows, fc2, 1, 1))[0].astype(BF)
    part_fc1 = line_sum(
        mm(normed, grad_hidden, 0, 0).astype(BF).reshape(shards, rows_here, hidden_cols)
    )

    qkv = mm(normed, qkv_w) + bias_qkv
    query, key, value = [
        qkv[:, i * head_cols : (i + 1) * head_cols].reshape(length, heads, HEAD_DIM)
        for i in range(3)
    ]
    query = rotate(query, cosine, sine).astype(BF)
    key = rotate(key, cosine, sine).astype(BF)
    value = value.astype(BF)
    mixed, grad_query, grad_key, grad_value = attention(
        query,
        key,
        value,
        lambda: mm(grad_rows, out_w, 1, 1).astype(BF).reshape(length, heads, HEAD_DIM),
        seg,
        score_scale,
    )
    mixed = mixed.reshape(length, head_cols)
    out_grad = mm(mixed, grad_rows, 0, 0).astype(BF)
    if strided:
        part_out = line_sum(out_grad.reshape(shards, each * HEAD_DIM, width))
    else:
        spread = jnp.zeros((seqs, head_cols, width), BF)
        spread = lax.dynamic_update_index_in_dim(spread, out_grad, me, 0)
        part_out = line_sum(spread.reshape(shards, shard_heads * HEAD_DIM, width))
    grad_qkv = jnp.concatenate(
        [rotate(grad_query, cosine, -sine), rotate(grad_key, cosine, -sine), grad_value], axis=1
    )
    grad_qkv = grad_qkv.reshape(length, 3 * head_cols).astype(BF)
    part_qkv = line_sum(
        mm(normed, grad_qkv, 0, 0).astype(BF).reshape(shards, rows_here, 3 * head_cols)
    )

    partial = (mm(mixed, out_w) + mm(active, fc2)).astype(BF)
    result = seq_sum(partial.reshape(seqs, tok, width))
    output = (inputs[0].astype(F32) + result + (bias_out + bias_fc2)).astype(BF)[None]

    grad_partial = mm(grad_qkv, qkv_w, 1, 1) + mm(grad_hidden, fc1, 1, 1)
    sum_gain = jnp.sum(grad_partial * normal_hat, axis=0)
    sum_shift = jnp.sum(grad_partial, axis=0)
    grad_normed = seq_sum(grad_partial.astype(BF).reshape(seqs, tok, width))
    own_hat = pick(normal_hat.reshape(seqs, tok, width), me)
    own_std = pick(inv_std.reshape(seqs, tok, 1), me)
    scaled = grad_normed * gain
    grad_in = cotangent[0].astype(F32) + own_std * (
        scaled
        - jnp.mean(scaled, axis=-1, keepdims=True)
        - own_hat * jnp.mean(scaled * own_hat, axis=-1, keepdims=True)
    )

    sum_fc1 = jnp.sum(grad_hidden.astype(F32), axis=0).reshape(shards, unit)
    sum_fc1 = lax.dynamic_update_index_in_dim(
        jnp.zeros((shards, seqs, unit), F32), sum_fc1, me, 1
    )
    sum_qkv = jnp.sum(grad_qkv.astype(F32), axis=0).reshape(3, heads, HEAD_DIM).transpose(1, 0, 2)
    if strided:
        sum_qkv = lax.dynamic_update_index_in_dim(
            jnp.zeros((shards, seqs, each, 3, HEAD_DIM), F32),
            sum_qkv.reshape(shards, each, 3, HEAD_DIM),
            me,
            1,
        )
    else:
        sum_qkv = lax.dynamic_update_index_in_dim(
            jnp.zeros((seqs, heads, 3, HEAD_DIM), F32), sum_qkv, me, 0
        )
    sum_out = jnp.sum(cotangent[0].astype(F32), axis=0)
    vectors = jnp.concatenate(
        [v.reshape(shards, -1) for v in (sum_gain, sum_shift, sum_out, sum_qkv, sum_fc1)], axis=1
    )
    vectors = line_sum(vectors[:, None, :])[0]
    vectors = jnp.sum(seq_gather(vectors[None]), axis=(0, 1))
    ends = [sizes[0], sizes[1], sizes[2], sizes[4], sizes[5]]
    ends = [sum(ends[:i]) for i in range(len(ends) + 1)]
    total_gain, total_shift, total_bout, total_bqkv, total_bfc1 = [
        vectors[a:b] for a, b in zip(ends[:-1], ends[1:])
    ]

    total_wfc2 = seq_gather(part_fc2.astype(BF)).reshape(seqs * unit, width).astype(F32)
    total_wfc1 = seq_gather(part_fc1.astype(BF)).reshape(seqs, rows_here, shards, unit)
    total_wfc1 = total_wfc1.transpose(1, 2, 0, 3).reshape(rows_here, -1).astype(F32)
    total_qkv = seq_gather(part_qkv.astype(BF))
    if strided:
        total_wout = seq_gather(part_out.astype(BF)).reshape(-1, width).astype(F32)
        total_qkv = total_qkv.reshape(seqs, rows_here, 3, shards, each, HEAD_DIM)
        total_qkv = total_qkv.transpose(1, 3, 0, 4, 2, 5)
    else:
        total_wout = jnp.sum(seq_gather(part_out.astype(BF)).astype(F32), axis=0)
        total_qkv = total_qkv.reshape(seqs, rows_here, 3, heads, HEAD_DIM).transpose(1, 0, 3, 2, 4)
    total_wqkv = total_qkv.reshape(rows_here, -1).astype(F32)
    return (
        output,
        grad_in[None],
        total_gain,
        total_shift,
        total_wqkv,
        total_bqkv,
        total_wout,
        total_bout,
        total_wfc1,
        total_bfc1,
        total_wfc2,
        total_bout,
    )


def solution(mesh):
    rows, vector, matrix = P("fsdp", "seq", None), P("fsdp"), P("fsdp", None)
    return jax.shard_map(
        per_device,
        mesh=mesh,
        in_specs=(
            rows,
            matrix,
            vector,
            vector,
            matrix,
            vector,
            matrix,
            vector,
            matrix,
            vector,
            matrix,
            vector,
            rows,
        ),
        out_specs=(
            rows,
            rows,
            vector,
            vector,
            matrix,
            vector,
            matrix,
            vector,
            matrix,
            vector,
            matrix,
            vector,
        ),
        check_vma=False,
    )
```

```python
import functools

import jax
import jax.numpy as jnp
from jax import lax
from jax.experimental import pallas as pl
from jax.experimental.pallas import tpu as pltpu
from jax.sharding import PartitionSpec as P

HEADS = 32
HEAD_DIM = 64
ROT = 32
EPS = 1e-05
BF = jnp.bfloat16
F32 = jnp.float32
VMEM_BYTES = 56 * 1024 * 1024


def mm(left, right, left_dim=1, right_dim=0):
    return lax.dot_general(
        left, right, (((left_dim,), (right_dim,)), ((), ())), preferred_element_type=F32
    )


def pick(array, index, axis=0):
    return lax.dynamic_index_in_dim(array, index, axis, keepdims=False)


def put(array, piece, index, axis=0):
    return lax.dynamic_update_index_in_dim(array, piece, index, axis)


def behind(array, other):
    first = lax.slice(other, (0,) * other.ndim, (1,) * other.ndim).reshape(())
    return jnp.where(jnp.isnan(first), jnp.zeros((), array.dtype), array)


def unread(arrays):
    return [pl.BlockSpec(memory_space=pl.ANY) for unused in arrays]


def params():
    return pltpu.CompilerParams(vmem_limit_bytes=VMEM_BYTES)


def cost(flops, size, transcendentals=0):
    return pl.CostEstimate(flops=flops, bytes_accessed=size, transcendentals=transcendentals)


def seq_exchange(blocks):
    return lax.all_to_all(blocks, "seq", split_axis=0, concat_axis=0)


def seq_gather(block):
    count = lax.axis_size("seq")
    return seq_exchange(jnp.broadcast_to(block[None], (count,) + block.shape))


def seq_gather_two(first, second):
    me, count = lax.axis_index("seq"), lax.axis_size("seq")
    bits = list(range(count.bit_length() - 1))
    orders = (bits, bits[::-1])
    wholes = [first[None], second[None]]
    for step in bits:
        got = []
        for whole, order in zip(wholes, orders):
            pairs = [(i, i ^ (1 << order[step])) for i in range(count)]
            got.append(lax.ppermute(whole, "seq", pairs))
        for i, order in enumerate(orders):
            low = (me >> order[step]) % 2 == 0
            whole, new = wholes[i], behind(got[i], got[1 - i])
            whole = jnp.where(low, jnp.stack([whole, new]), jnp.stack([new, whole]))
            wholes[i] = whole.reshape((-1,) + first.shape)
    sizes = (2,) * len(bits) + second.shape
    order = bits[::-1] + [len(bits) + i for i in range(second.ndim)]
    return wholes[0], wholes[1].reshape(sizes).transpose(order).reshape(wholes[1].shape)


def seq_all(block):
    return lax.all_gather(block, "seq", axis=0)


def seq_sum(blocks):
    return jnp.sum(seq_exchange(blocks).astype(F32), axis=0)


def fsdp_place():
    me = lax.axis_index("fsdp")
    return lax.axis_size("fsdp") // 2, me // 2, me % 2


def to_chips(array, moves):
    pairs = [(2 * a + core, 2 * b + core) for a, b in moves for core in (0, 1)]
    return lax.ppermute(array, "fsdp", pairs)


def to_other_core(array):
    count = lax.axis_size("fsdp")
    return lax.ppermute(array, "fsdp", [(i, i ^ 1) for i in range(count)])


def fsdp_gather(block):
    return lax.all_gather(block, "fsdp", axis=0, tiled=True)


class LineSum:
    def __init__(self, other, own_of):
        chips, chip, core = fsdp_place()
        own = own_of(to_other_core(other))
        first = jnp.where(chip == 0, own[chips - 1], own[1])
        got = to_chips(first, [(chips - 1, chips - 2), (0, 1)])
        self.first = first
        self.steps = [own, got]
        total = own[0].astype(F32) + got.astype(F32)
        down, up = got, got
        for step in range(2, chips):
            down = (down.astype(F32) + own[step].astype(F32)).astype(own.dtype)
            up = (up.astype(F32) + own[chips - step].astype(F32)).astype(own.dtype)
            down = to_chips(down, [(a, a - 1) for a in range(chips - step, chips)])
            up = to_chips(up, [(a, a + 1) for a in range(0, step)])
            self.steps += [down, up]
        if chips > 2:
            total = own[0].astype(F32) + down.astype(F32) + up.astype(F32)
        self.total = total


def attention_kernel(rows, half, qkv_ref, grad_ref, cos_ref, sin_ref, open_ref, *refs):
    mixed_ref, out_ref, key_ref, value_ref = refs[-4:]
    length = qkv_ref.shape[0]
    wide = 2 * half
    lane = lax.broadcasted_iota(jnp.int32, (length, wide), 1)
    turned = ROT // 2
    leading = (lane % half) < turned
    cosine, sine = cos_ref[...], sin_ref[...]
    scale = half ** (-0.5)

    def turn(x, s):
        other = jnp.where(leading, pltpu.roll(x, wide - turned, 1), pltpu.roll(x, turned, 1))
        return x * cosine + other * s

    query = turn(qkv_ref[:, :wide], sine).astype(BF)
    key = turn(qkv_ref[:, wide : 2 * wide], sine).astype(BF)
    value = qkv_ref[:, 2 * wide :].astype(BF)
    query = (query.astype(F32) * scale).astype(BF)
    grad = grad_ref[...]
    key_t = key.astype(F32).T.astype(BF)
    value_t = value.astype(F32).T.astype(BF)
    key_ref[...] = jnp.zeros_like(key_ref)
    value_ref[...] = jnp.zeros_like(value_ref)
    zero = jnp.zeros((), BF)
    for begin in range(0, length, rows):
        end = begin + rows
        cut = slice(begin, end)
        k_pos = lax.broadcasted_iota(jnp.int32, (end, rows), 0)
        q_pos = lax.broadcasted_iota(jnp.int32, (end, rows), 1) + begin
        allowed = (k_pos <= q_pos) & (k_pos >= open_ref[:, cut])
        side = lane[:rows] < half
        mixed_t, query_t = [], []
        for head in range(2):
            here = side if head == 0 else ~side
            q_rows = jnp.where(here, query[cut], zero)
            g_rows = jnp.where(here, grad[cut], zero)
            scores = jnp.where(allowed, mm(key[:end], q_rows, 1, 1), -1000000000.0)
            expo = jnp.exp(scores - jnp.max(scores, axis=0, keepdims=True))
            probs = expo * (1.0 / jnp.sum(expo, axis=0, keepdims=True))
            low = probs.astype(BF)
            own = slice(head * half, (head + 1) * half)
            mixed_t.append(mm(value_t[own, :end], low))
            grad_probs = mm(value[:end], g_rows, 1, 1)
            dots = jnp.sum(probs * grad_probs, axis=0, keepdims=True)
            grad_scores = (probs * (grad_probs - dots)).astype(BF)
            query_t.append(mm(key_t[own, :end], grad_scores))
            key_ref[:end] += mm(grad_scores, q_rows)
            value_ref[:end] += mm(low, g_rows)
        mixed_ref[cut] = jnp.concatenate(mixed_t, axis=0).T.astype(BF)
        q_grad = jnp.concatenate(query_t, axis=0).T * scale
        lead = leading[:rows]
        other = jnp.where(
            lead, pltpu.roll(q_grad, wide - turned, 1), pltpu.roll(q_grad, turned, 1)
        )
        out_ref[cut, :wide] = (q_grad * cosine[cut] - other * sine[cut]).astype(BF)
    out_ref[:, wide : 2 * wide] = turn(key_ref[...], -sine).astype(BF)
    out_ref[:, 2 * wide :] = value_ref[...].astype(BF)


def attention(qkv, grad, cosine, sine, opening, begin, steps, before=(), after=()):
    length = qkv.shape[0]
    wide = 2 * HEAD_DIM
    pairs = grad.shape[1] // wide

    def whole(array):
        return pl.BlockSpec(array.shape, lambda p: (0, 0))

    narrow = pl.BlockSpec((length, wide), lambda p: (0, begin + p))
    three = pl.BlockSpec((length, 3 * wide), lambda p: (0, begin + p))
    return pl.pallas_call(
        functools.partial(attention_kernel, min(256, length), HEAD_DIM),
        grid=(steps,),
        in_specs=[three, narrow, whole(cosine), whole(sine), whole(opening)]
        + unread(before)
        + unread(after),
        out_specs=[narrow, three],
        out_shape=[
            jax.ShapeDtypeStruct((length, pairs * wide), BF),
            jax.ShapeDtypeStruct((length, pairs * 3 * wide), BF),
        ],
        input_output_aliases={5 + i: i for i in range(len(before))},
        scratch_shapes=[pltpu.VMEM((length, wide), F32), pltpu.VMEM((length, wide), F32)],
        compiler_params=params(),
        cost_estimate=cost(
            24 * length * length * wide * steps,
            24 * length * wide * steps,
            length * length * steps,
        ),
    )(qkv, grad, cosine, sine, opening, *before, *after)


def norm_kernel(in_ref, gain_ref, shift_ref, out_ref, mean_ref, std_ref):
    value = in_ref[...].astype(F32)
    mean = jnp.mean(value, axis=-1, keepdims=True)
    centred = value - mean
    std = lax.rsqrt(jnp.mean(centred * centred, axis=-1, keepdims=True) + EPS)
    out_ref[...] = (centred * std * gain_ref[...] + shift_ref[...]).astype(BF)
    mean_ref[...] = mean
    std_ref[...] = std


def layer_norm(rows_in, gain, shift):
    rows, columns = rows_in.shape
    cut = min(256, rows)
    block = pl.BlockSpec((cut, columns), lambda i: (i, 0))
    vector = pl.BlockSpec((1, columns), lambda i: (0, 0))
    narrow = pl.BlockSpec((cut, 1), lambda i: (i, 0))
    return pl.pallas_call(
        norm_kernel,
        grid=(rows // cut,),
        in_specs=[block, vector, vector],
        out_specs=[block, narrow, narrow],
        out_shape=[
            jax.ShapeDtypeStruct((rows, columns), BF),
            jax.ShapeDtypeStruct((rows, 1), F32),
            jax.ShapeDtypeStruct((rows, 1), F32),
        ],
        compiler_params=params(),
        cost_estimate=cost(10 * rows * columns, 4 * rows * columns),
    )(rows_in, gain[None], shift[None])


def mixed_kernel(cut, high, left_ref, both_ref, *refs):
    weight_ref, out_ref = refs[-2:]
    wide = both_ref.shape[1]
    for i in range(both_ref.shape[0] // high):
        rows = slice(i // cut * high, (i // cut + 1) * high)
        columns = slice(i % cut * wide, (i % cut + 1) * wide)
        weight_ref[rows, columns] = both_ref[i * high : (i + 1) * high, :]
    out_ref[...] = mm(left_ref[...], weight_ref[...], 1, 1).astype(BF)


def mixed_gradient(left, both, begin, cut, high, after=()):
    rows, depth = left.shape
    wide = depth // cut
    weight = (both.shape[0] // cut, depth)

    def whole(shape):
        return pl.BlockSpec(shape, lambda i: (0, 0))

    return pl.pallas_call(
        functools.partial(mixed_kernel, cut, high),
        grid=(1,),
        in_specs=[
            whole(left.shape),
            pl.BlockSpec((both.shape[0], wide), lambda i: (0, begin // wide)),
        ]
        + unread(after),
        out_specs=[whole(weight), whole((rows, weight[0]))],
        out_shape=[
            jax.ShapeDtypeStruct(weight, BF),
            jax.ShapeDtypeStruct((rows, weight[0]), BF),
        ],
        compiler_params=params(),
        cost_estimate=cost(2 * rows * depth * weight[0], 4 * rows * depth),
    )(left, both, *after)


def hidden_kernel(left_ref, right_ref, bias_ref, active_ref, slope_ref):
    value = mm(left_ref[...], right_ref[...]) + bias_ref[...]
    square = value * value
    scaled = 0.7978845608028654 * value
    bend = 0.044715 * square
    tanh = jnp.tanh(scaled * (1.0 + bend))
    half = 0.5 * (1.0 + tanh)
    active_ref[...] = (value * half).astype(BF)
    slope = half + 0.5 * (1.0 - tanh * tanh) * scaled * (1.0 + 3.0 * bend)
    slope_ref[...] = slope.astype(BF)


def hidden_layer(left, right, bias):
    rows, depth = left.shape
    columns = right.shape[1]
    cut = min(512, columns)
    block = pl.BlockSpec((rows, cut), lambda j: (0, j))
    return pl.pallas_call(
        hidden_kernel,
        grid=(columns // cut,),
        in_specs=[
            pl.BlockSpec((rows, depth), lambda j: (0, 0)),
            pl.BlockSpec((depth, cut), lambda j: (0, j)),
            pl.BlockSpec((1, cut), lambda j: (0, j)),
        ],
        out_specs=[block, block],
        out_shape=[jax.ShapeDtypeStruct((rows, columns), BF)] * 2,
        compiler_params=params(),
        cost_estimate=cost(2 * rows * depth * columns, 4 * rows * (depth + columns), rows * columns),
    )(left, right, bias[None])


def term_kernel(adds, index_ref, left_ref, right_ref, *refs):
    value = mm(left_ref[...], right_ref[...], 0, 0)
    if adds:
        value = value + refs[0][0].astype(F32)
    refs[-1][0] = value.astype(BF)


def block_terms(left, right, width, index, add=None, after=()):
    rows, columns = right.shape
    count = len(index)
    if width % 128:
        blocks = [lax.dynamic_slice_in_dim(left, i * width, width, 1) for i in index]
        value = jnp.stack([mm(block, right, 0, 0) for block in blocks])
        return (value if add is None else value + add.astype(F32)).astype(BF)
    index = jnp.stack([jnp.asarray(i, jnp.int32) for i in index])
    adds = [] if add is None else [add]
    out = pl.BlockSpec((1, width, columns), lambda r, index: (r, 0, 0))
    return pl.pallas_call(
        functools.partial(term_kernel, len(adds)),
        grid_spec=pltpu.PrefetchScalarGridSpec(
            num_scalar_prefetch=1,
            grid=(count,),
            in_specs=[
                pl.BlockSpec((rows, width), lambda r, index: (0, index[r])),
                pl.BlockSpec((rows, columns), lambda r, index: (0, 0)),
            ]
            + [out] * len(adds)
            + unread(after),
            out_specs=out,
        ),
        out_shape=jax.ShapeDtypeStruct((count, width, columns), BF),
        compiler_params=params(),
        cost_estimate=cost(2 * rows * width * count * columns, 4 * rows * columns),
    )(index, left, right, *adds, *after)


def two_terms_kernel(cut, adds, index_ref, left_ref, right_ref, beside_ref, *refs):
    out_ref = refs[-1]
    columns = right_ref.shape[1]
    value = mm(left_ref[...], right_ref[...], 0, 0)
    if adds:
        value = value + refs[0][0, :, :columns].astype(F32)
    out_ref[0, :, :columns] = value.astype(BF)
    high = beside_ref.shape[1]
    wide = beside_ref.shape[2] // cut
    for i in range(cut):
        part = slice(i * high, (i + 1) * high)
        value = beside_ref[0, :, i * wide : (i + 1) * wide]
        if adds:
            value = (value.astype(F32) + refs[0][0, part, columns:].astype(F32)).astype(BF)
        out_ref[0, part, columns:] = value


def two_terms(left, right, width, beside, cut, index, add=None, after=()):
    rows, columns = right.shape
    count = len(index)
    extra = beside.shape[2] // cut
    index = jnp.stack([jnp.asarray(i, jnp.int32) for i in index])
    adds = [] if add is None else [add]
    out = pl.BlockSpec((1, width, columns + extra), lambda r, index: (r, 0, 0))
    return pl.pallas_call(
        functools.partial(two_terms_kernel, cut, len(adds)),
        grid_spec=pltpu.PrefetchScalarGridSpec(
            num_scalar_prefetch=1,
            grid=(count,),
            in_specs=[
                pl.BlockSpec((rows, width), lambda r, index: (0, index[r])),
                pl.BlockSpec((rows, columns), lambda r, index: (0, 0)),
                pl.BlockSpec((1,) + beside.shape[1:], lambda r, index: (index[r], 0, 0)),
            ]
            + [out] * len(adds)
            + unread(after),
            out_specs=out,
        ),
        out_shape=jax.ShapeDtypeStruct((count, width, columns + extra), BF),
        compiler_params=params(),
        cost_estimate=cost(2 * rows * width * count * columns, 4 * rows * columns),
    )(index, left, right, beside, *adds, *after)


def product_kernel(left_ref, right_ref, bias_ref, *refs):
    refs[-1][...] = mm(left_ref[...], right_ref[...]) + bias_ref[...]


def product(left, right, bias, after=()):
    rows, depth = left.shape
    columns = bias.shape[0]
    cut = 512 if columns % 512 == 0 else 256
    return pl.pallas_call(
        product_kernel,
        grid=(columns // cut,),
        in_specs=[
            pl.BlockSpec((rows, depth), lambda j: (0, 0)),
            pl.BlockSpec((depth, cut), lambda j: (0, j)),
            pl.BlockSpec((1, cut), lambda j: (0, j)),
        ]
        + unread(after),
        out_specs=pl.BlockSpec((rows, cut), lambda j: (0, j)),
        out_shape=jax.ShapeDtypeStruct((rows, columns), F32),
        compiler_params=params(),
        cost_estimate=cost(2 * rows * depth * columns, 4 * rows * (depth + columns)),
    )(left, right, bias[None], *after)


def slope_kernel(left_ref, right_ref, slope_ref, *refs):
    value = mm(left_ref[...], right_ref[...], 1, 1) * slope_ref[...].astype(F32)
    refs[-1][...] = value.astype(BF)


def times_slope(left, right, slope, after=()):
    rows, depth = left.shape
    columns = right.shape[0]
    cut = min(512, columns)
    block = pl.BlockSpec((rows, cut), lambda j: (0, j))
    return pl.pallas_call(
        slope_kernel,
        grid=(columns // cut,),
        in_specs=[
            pl.BlockSpec((rows, depth), lambda j: (0, 0)),
            pl.BlockSpec((cut, depth), lambda j: (j, 0)),
            block,
        ]
        + unread(after),
        out_specs=block,
        out_shape=jax.ShapeDtypeStruct(slope.shape, BF),
        compiler_params=params(),
        cost_estimate=cost(2 * rows * depth * columns, 6 * rows * depth),
    )(left, right, slope, *after)


def output_kernel(left_ref, right_ref, second_ref, weight_ref, *refs):
    value = mm(left_ref[...], right_ref[...]) + mm(second_ref[...], weight_ref[...])
    refs[-1][...] = value.astype(BF)


def output_terms(left, right, second, weight, after=()):
    rows, depth = left.shape
    columns = right.shape[1]
    cut = min(512, columns)
    return pl.pallas_call(
        output_kernel,
        grid=(columns // cut,),
        in_specs=[
            pl.BlockSpec((rows, depth), lambda j: (0, 0)),
            pl.BlockSpec((depth, cut), lambda j: (0, j)),
            pl.BlockSpec(second.shape, lambda j: (0, 0)),
            pl.BlockSpec((second.shape[1], cut), lambda j: (0, j)),
        ]
        + unread(after),
        out_specs=pl.BlockSpec((rows, cut), lambda j: (0, j)),
        out_shape=jax.ShapeDtypeStruct((rows, columns), BF),
        compiler_params=params(),
        cost_estimate=cost(2 * rows * (depth + second.shape[1]) * columns, 6 * rows * depth),
    )(left, right, second, weight, *after)


def normed_kernel(one_ref, first_ref, two_ref, second_ref, in_ref, mean_ref, std_ref, *refs):
    out_ref, gain_ref, shift_ref = refs[-3:]
    value = mm(one_ref[...], first_ref[...], 1, 1) + mm(two_ref[...], second_ref[...], 1, 1)
    out_ref[...] = value.astype(BF)
    normal_hat = (in_ref[...].astype(F32) - mean_ref[...]) * std_ref[...]
    gain_ref[...] = jnp.sum(value * normal_hat, axis=0, keepdims=True)
    shift_ref[...] = jnp.sum(value, axis=0, keepdims=True)


def normed_terms(one, first, two, second, rows_in, mean, std, after=()):
    rows = one.shape[0]
    columns = first.shape[0]
    cut = min(512, columns)
    vector = pl.BlockSpec((1, cut), lambda j: (0, j))

    def whole(array):
        return pl.BlockSpec(array.shape, lambda j: (0, 0))

    return pl.pallas_call(
        normed_kernel,
        grid=(columns // cut,),
        in_specs=[
            whole(one),
            pl.BlockSpec((cut, one.shape[1]), lambda j: (j, 0)),
            whole(two),
            pl.BlockSpec((cut, second.shape[1]), lambda j: (j, 0)),
            pl.BlockSpec((rows, cut), lambda j: (0, j)),
            whole(mean),
            whole(std),
        ]
        + unread(after),
        out_specs=[pl.BlockSpec((rows, cut), lambda j: (0, j)), vector, vector],
        out_shape=[
            jax.ShapeDtypeStruct((rows, columns), BF),
            jax.ShapeDtypeStruct((1, columns), F32),
            jax.ShapeDtypeStruct((1, columns), F32),
        ],
        compiler_params=params(),
        cost_estimate=cost(2 * rows * columns * (one.shape[1] + two.shape[1]), 8 * rows * columns),
    )(one, first, two, second, rows_in, mean, std, *after)


def spread_kernel(width, in_ref, out_ref):
    for s in range(in_ref.shape[0]):
        out_ref[:, s * width : (s + 1) * width] = in_ref[s].astype(F32)


def spread_columns(pieces, width):
    count, rows, columns = pieces.shape
    return pl.pallas_call(
        functools.partial(spread_kernel, width),
        grid=(columns // width,),
        in_specs=[pl.BlockSpec((count, rows, width), lambda i: (0, 0, i))],
        out_specs=pl.BlockSpec((rows, width * count), lambda i: (0, i)),
        out_shape=jax.ShapeDtypeStruct((rows, columns * count), F32),
        compiler_params=params(),
        cost_estimate=cost(0, 6 * rows * columns * count),
    )(pieces)


def heads_kernel(half, in_ref, out_ref):
    parts = []
    for head in range(2):
        for s in range(in_ref.shape[0]):
            for part in range(3):
                start = (2 * part + head) * half
                parts.append(in_ref[s, :, start : start + half].astype(F32))
    for i in range(0, len(parts), 2):
        out_ref[:, i * half : (i + 2) * half] = jnp.concatenate(parts[i : i + 2], axis=1)


def spread_heads(pieces, pairs):
    count, rows, unused = pieces.shape
    width = 6 * HEAD_DIM
    return pl.pallas_call(
        functools.partial(heads_kernel, HEAD_DIM),
        grid=(pairs,),
        in_specs=[pl.BlockSpec((count, rows, width), lambda i: (0, 0, i))],
        out_specs=pl.BlockSpec((rows, width * count), lambda i: (0, i)),
        out_shape=jax.ShapeDtypeStruct((rows, pairs * width * count), F32),
        compiler_params=params(),
        cost_estimate=cost(0, 6 * rows * pairs * width * count),
    )(pieces)


def by_pairs(array, heads):
    lead = array.shape[:-1]
    array = array.reshape(lead + (heads // 2, 2, 3, HEAD_DIM))
    return jnp.swapaxes(array, -3, -2).reshape(lead + (heads * 3 * HEAD_DIM,))


def by_heads(array, heads):
    lead = array.shape[:-1]
    array = array.reshape(lead + (heads // 2, 3, 2, HEAD_DIM))
    return jnp.swapaxes(array, -3, -2).reshape(lead + (heads * 3 * HEAD_DIM,))


def per_device(
    inputs,
    doc_starts,
    ln_gain,
    ln_bias,
    w_qkv,
    b_qkv,
    w_out,
    b_out,
    w_fc1,
    b_fc1,
    w_fc2,
    b_fc2,
    cotangent,
):
    seqs, shards = lax.axis_size("seq"), lax.axis_size("fsdp")
    me = lax.axis_index("seq")
    chips, chip, core = fsdp_place()
    tok, width = inputs.shape[1:]
    length = tok * seqs
    rows_here = w_qkv.shape[0]
    heads = HEADS // seqs
    head_cols = heads * HEAD_DIM
    shard_heads = w_out.shape[0] // HEAD_DIM
    strided = shard_heads % seqs == 0
    each = shard_heads // seqs
    unit = w_fc2.shape[0] // seqs
    hidden_cols = unit * shards
    order = [2 * ((chip + r) % chips) + (core ^ h) for h in (0, 1) for r in range(chips)]

    fc1_here = jnp.concatenate(
        [
            lax.dynamic_slice_in_dim(w_fc1, (i * seqs + me) * unit, unit, 1)
            for i in range(shards)
        ],
        axis=1,
    )
    fc2_here = pick(w_fc2.reshape(seqs, unit, width), me)
    if strided:
        qkv_here = pick(w_qkv.reshape(rows_here, shards, seqs, each * 3 * HEAD_DIM), me, 2)
    else:
        qkv_here = pick(w_qkv.reshape(rows_here, seqs, heads * 3 * HEAD_DIM), me, 1)
    qkv_here = by_pairs(qkv_here.reshape(rows_here, 3 * head_cols), heads)
    out_cut = rows_here // (each * HEAD_DIM) if strided else 1
    if strided:
        out_here = pick(w_out.reshape(seqs, each * HEAD_DIM, width), me)
        out_here = out_here.reshape(each * HEAD_DIM, out_cut, width // out_cut)
        out_here = jnp.swapaxes(out_here, 0, 1).reshape(rows_here, width // out_cut)
        qkv_here = jnp.concatenate([qkv_here, out_here], axis=1)

    sizes = [v.shape[0] for v in (ln_gain, ln_bias, b_out, b_fc2, b_qkv, b_fc1)]
    small = jnp.concatenate([ln_gain, ln_bias, b_out, b_fc2, b_qkv, b_fc1])[None]
    small = lax.all_gather(small, "fsdp", axis=0, tiled=True).astype(F32)
    cuts = [sum(sizes[:i]) for i in range(len(sizes) + 1)]
    gain, shift, bias_out, bias_fc2, bias_qkv, bias_fc1 = [
        small[:, a:b].reshape(-1) for a, b in zip(cuts[:-1], cuts[1:])
    ]
    bias_fc1 = pick(bias_fc1.reshape(shards, seqs, unit), me, 1).reshape(hidden_cols)
    if strided:
        bias_qkv = pick(bias_qkv.reshape(shards, seqs, each * 3 * HEAD_DIM), me, 1)
    else:
        bias_qkv = pick(bias_qkv.reshape(seqs, heads * 3 * HEAD_DIM), me)
    bias_qkv = by_pairs(bias_qkv.reshape(3 * head_cols), heads)

    fc1 = fsdp_gather(fc1_here)
    rows_all, grad_rows = seq_gather_two(inputs[0], cotangent[0])
    rows_all, grad_rows = rows_all.reshape(length, width), grad_rows.reshape(length, width)

    starts_row = doc_starts[0]
    pos = jnp.arange(length, dtype=jnp.int32)
    before = starts_row[None, :] <= pos[:, None]
    opening = jnp.max(jnp.where(before, starts_row[None, :], 0), axis=1)
    rates = 10000.0 ** (-2.0 * jnp.arange(ROT // 2, dtype=F32) / ROT)
    angle = (pos - opening).astype(F32)[:, None] * rates[None, :]
    cosine, sine = jnp.cos(angle), jnp.sin(angle)
    rest = jnp.ones((length, HEAD_DIM - ROT), F32)
    cosine = jnp.concatenate([cosine, cosine, rest] * 2, axis=1)
    sine = jnp.concatenate([-sine, sine, 0.0 * rest] * 2, axis=1)

    normed, mean, inv_std = layer_norm(rows_all, behind(gain, grad_rows), shift)
    both = fsdp_gather(behind(qkv_here, normed))
    mine, others = order[:chips], order[chips:]

    active, slope = hidden_layer(normed, fc1, bias_fc1)
    other_fc2 = block_terms(active, grad_rows, unit, others)
    sum_fc2 = LineSum(other_fc2, lambda got: block_terms(active, grad_rows, unit, mine, got))
    fc2 = fsdp_gather(behind(fc2_here, sum_fc2.first))

    ahead = sum_fc2.steps[1:2]
    if strided:
        high = each * HEAD_DIM
        out_w, grad_mixed = mixed_gradient(grad_rows, both, 3 * head_cols, out_cut, high, ahead)
    else:
        out_w = pick(fsdp_gather(w_out).reshape(seqs, head_cols, width), me)
        grad_mixed = mm(grad_rows, out_w, 1, 1).astype(BF)
    qkv = product(normed, both, bias_qkv, [grad_mixed])
    tables = (cosine, sine, opening[None])
    pairs = heads // 2
    early = attention(qkv, grad_mixed, *tables, 0, pairs // 2)
    mixed, grad_qkv = attention(
        qkv, grad_mixed, *tables, pairs // 2, pairs - pairs // 2, early, sum_fc2.steps[2:4]
    )
    out_grad = mm(mixed, grad_rows, 0, 0).astype(BF)
    ahead = sum_fc2.steps[4:6]
    if strided:
        out_grad = out_grad.reshape(shards, each * HEAD_DIM, width)

        def qkv_terms(index, add=None, after=()):
            return two_terms(normed, grad_qkv, rows_here, out_grad, out_cut, index, add, after)

    else:
        spread = put(jnp.zeros((seqs, head_cols, width), BF), out_grad, me)
        spread = spread.reshape(shards, shard_heads * HEAD_DIM, width)
        part_out = LineSum(
            jnp.stack([pick(spread, i) for i in others]),
            lambda got: jnp.stack([pick(spread, i) for i in mine]) + got,
        ).total

        def qkv_terms(index, add=None, after=()):
            return block_terms(normed, grad_qkv, rows_here, index, add, after)

    other_qkv = qkv_terms(others, None, ahead)
    grad_hidden = times_slope(grad_rows, fc2, slope, [other_qkv])
    sum_qkv = LineSum(other_qkv, lambda got: qkv_terms(mine, got, [grad_hidden]))
    other_fc1 = block_terms(normed, grad_hidden, rows_here, others, None, sum_qkv.steps[:1])
    partial = output_terms(active, fc2, mixed, out_w, [other_fc1])
    grad_partial, sum_gain, sum_shift = normed_terms(
        grad_qkv,
        both,
        grad_hidden,
        fc1,
        rows_all,
        mean,
        inv_std,
        [partial] + sum_qkv.steps[1:2],
    )
    sum_fc1 = LineSum(
        other_fc1,
        lambda got: block_terms(
            normed, grad_hidden, rows_here, mine, got, sum_qkv.steps[2:4] + [grad_partial]
        ),
    )
    result = seq_sum(partial.reshape(seqs, tok, width))
    grad_normed = seq_sum(grad_partial.reshape(seqs, tok, width))
    whole_fc2 = seq_all(sum_fc2.total.astype(BF))
    total = behind(sum_qkv.total.astype(BF), sum_fc1.steps[1])
    whole_qkv = seq_all(behind(total, result))
    whole_fc1 = seq_all(behind(sum_fc1.total.astype(BF), grad_normed))
    output = (inputs[0].astype(F32) + result + (bias_out + bias_fc2)).astype(BF)[None]
    sum_gain, sum_shift = sum_gain[0], sum_shift[0]
    own_std = pick(inv_std.reshape(seqs, tok, 1), me)
    own_hat = (inputs[0].astype(F32) - pick(mean.reshape(seqs, tok, 1), me)) * own_std
    scaled = grad_normed * gain
    grad_in = own_std * (
        scaled
        - jnp.mean(scaled, axis=-1, keepdims=True)
        - own_hat * jnp.mean(scaled * own_hat, axis=-1, keepdims=True)
    )
    grad_in = cotangent[0].astype(F32) + grad_in

    sum_bfc1 = jnp.sum(grad_hidden.astype(F32), axis=0).reshape(shards, unit)
    sum_bfc1 = put(jnp.zeros((shards, seqs, unit), F32), sum_bfc1, me, 1)
    sum_bqkv = by_heads(jnp.sum(grad_qkv.astype(F32), axis=0), heads)
    if strided:
        sum_bqkv = sum_bqkv.reshape(shards, each * 3 * HEAD_DIM)
        sum_bqkv = put(jnp.zeros((shards, seqs, each * 3 * HEAD_DIM), F32), sum_bqkv, me, 1)
    else:
        sum_bqkv = put(jnp.zeros((seqs, heads * 3 * HEAD_DIM), F32), sum_bqkv, me)
    sum_out = jnp.sum(cotangent[0].astype(F32), axis=0)
    vectors = jnp.concatenate(
        [v.reshape(shards, -1) for v in (sum_gain, sum_shift, sum_out, sum_bqkv, sum_bfc1)], axis=1
    )
    vectors = vectors[:, None]
    vectors = LineSum(
        jnp.stack([pick(vectors, i) for i in others]),
        lambda got: jnp.stack([pick(vectors, i) for i in mine]) + got,
    ).total
    vectors = jnp.sum(seq_gather(vectors), axis=(0, 1))
    ends = [sizes[0], sizes[1], sizes[2], sizes[4], sizes[5]]
    ends = [sum(ends[:i]) for i in range(len(ends) + 1)]
    total_gain, total_shift, total_bout, total_bqkv, total_bfc1 = [
        vectors[a:b] for a, b in zip(ends[:-1], ends[1:])
    ]

    total_wfc2 = whole_fc2.astype(F32).reshape(seqs * unit, width)
    if unit % 128 == 0:
        total_wfc1 = spread_columns(whole_fc1, unit)
    else:
        total_wfc1 = whole_fc1.astype(F32).reshape(seqs, rows_here, shards, unit)
        total_wfc1 = total_wfc1.transpose(1, 2, 0, 3).reshape(rows_here, -1)
    if strided and each == 1:
        total_wqkv = spread_heads(whole_qkv, heads // 2)
    else:
        total_wqkv = by_heads(whole_qkv[:, :, : 3 * head_cols].astype(F32), heads)
        if strided:
            total_wqkv = total_wqkv.reshape(seqs, rows_here, shards, each * 3 * HEAD_DIM)
            total_wqkv = total_wqkv.transpose(1, 2, 0, 3).reshape(rows_here, -1)
        else:
            total_wqkv = total_wqkv.transpose(1, 0, 2).reshape(rows_here, -1)
    if strided:
        total_wout = whole_qkv[:, :, 3 * head_cols :].astype(F32)
        total_wout = total_wout.reshape(seqs, out_cut, each * HEAD_DIM, width // out_cut)
        total_wout = jnp.swapaxes(total_wout, 1, 2).reshape(-1, width)
    else:
        total_wout = jnp.sum(seq_all(part_out.astype(BF)).astype(F32), axis=0)
    return (
        output,
        grad_in[None],
        total_gain,
        total_shift,
        total_wqkv,
        total_bqkv,
        total_wout,
        total_bout,
        total_wfc1,
        total_bfc1,
        total_wfc2,
        total_bout,
    )


def solution(mesh):
    rows, vector, matrix = P("fsdp", "seq", None), P("fsdp"), P("fsdp", None)
    weights = (vector, vector) + (matrix, vector) * 4
    return jax.shard_map(
        per_device,
        mesh=mesh,
        in_specs=(rows, matrix) + weights + (rows,),
        out_specs=(rows, rows) + weights,
        check_vma=False,
    )
```

```python
import functools

import jax
import jax.numpy as jnp
from jax import lax
from jax.experimental import pallas as pl
from jax.experimental.pallas import tpu as pltpu
from jax.sharding import PartitionSpec as P

HEADS = 32
HEAD_DIM = 64
ROT = 32
EPS = 1e-05
BF = jnp.bfloat16
F32 = jnp.float32
VMEM_BYTES = 56 * 1024 * 1024


def mm(left, right, left_dim=1, right_dim=0):
    return lax.dot_general(
        left, right, (((left_dim,), (right_dim,)), ((), ())), preferred_element_type=F32
    )


def pick(array, index, axis=0):
    return lax.dynamic_index_in_dim(array, index, axis, keepdims=False)


def put(array, piece, index, axis=0):
    return lax.dynamic_update_index_in_dim(array, piece, index, axis)


def behind(array, other):
    first = lax.slice(other, (0,) * other.ndim, (1,) * other.ndim).reshape(())
    return jnp.where(jnp.isnan(first), jnp.zeros((), array.dtype), array)


def unread(arrays):
    return [pl.BlockSpec(memory_space=pl.ANY) for unused in arrays]


def params():
    return pltpu.CompilerParams(vmem_limit_bytes=VMEM_BYTES)


def cost(flops, size, transcendentals=0):
    return pl.CostEstimate(flops=flops, bytes_accessed=size, transcendentals=transcendentals)


def seq_exchange(blocks):
    return lax.all_to_all(blocks, "seq", split_axis=0, concat_axis=0)


def seq_gather(block):
    count = lax.axis_size("seq")
    return seq_exchange(jnp.broadcast_to(block[None], (count,) + block.shape))


def seq_gather_two(first, second):
    me, count = lax.axis_index("seq"), lax.axis_size("seq")
    bits = list(range(count.bit_length() - 1))
    orders = (bits, bits[::-1])
    wholes = [first[None], second[None]]
    for step in bits:
        got = []
        for whole, order in zip(wholes, orders):
            pairs = [(i, i ^ (1 << order[step])) for i in range(count)]
            got.append(lax.ppermute(whole, "seq", pairs))
        for i, order in enumerate(orders):
            low = (me >> order[step]) % 2 == 0
            whole, new = wholes[i], behind(got[i], got[1 - i])
            whole = jnp.where(low, jnp.stack([whole, new]), jnp.stack([new, whole]))
            wholes[i] = whole.reshape((-1,) + first.shape)
    sizes = (2,) * len(bits) + second.shape
    order = bits[::-1] + [len(bits) + i for i in range(second.ndim)]
    return wholes[0], wholes[1].reshape(sizes).transpose(order).reshape(wholes[1].shape)


def seq_all(block):
    return lax.all_gather(block, "seq", axis=0)


def seq_sum(blocks):
    return jnp.sum(seq_exchange(blocks).astype(F32), axis=0)


def fsdp_place():
    me = lax.axis_index("fsdp")
    return lax.axis_size("fsdp") // 2, me // 2, me % 2


def to_chips(array, moves):
    pairs = [(2 * a + core, 2 * b + core) for a, b in moves for core in (0, 1)]
    return lax.ppermute(array, "fsdp", pairs)


def to_other_core(array):
    count = lax.axis_size("fsdp")
    return lax.ppermute(array, "fsdp", [(i, i ^ 1) for i in range(count)])


def fsdp_gather(block):
    return lax.all_gather(block, "fsdp", axis=0, tiled=True)


def fsdp_sum(parts):
    return lax.psum_scatter(parts, "fsdp", scatter_dimension=0, tiled=True)


class LineSum:
    def __init__(self, other, own_of):
        chips, chip, core = fsdp_place()
        own = own_of(to_other_core(other))
        first = jnp.where(chip == 0, own[chips - 1], own[1])
        got = to_chips(first, [(chips - 1, chips - 2), (0, 1)])
        self.first = first
        self.steps = [own, got]
        total = own[0].astype(F32) + got.astype(F32)
        down, up = got, got
        for step in range(2, chips):
            down = (down.astype(F32) + own[step].astype(F32)).astype(own.dtype)
            up = (up.astype(F32) + own[chips - step].astype(F32)).astype(own.dtype)
            down = to_chips(down, [(a, a - 1) for a in range(chips - step, chips)])
            up = to_chips(up, [(a, a + 1) for a in range(0, step)])
            self.steps += [down, up]
        if chips > 2:
            total = own[0].astype(F32) + down.astype(F32) + up.astype(F32)
        self.total = total


def attention_kernel(rows, half, qkv_ref, grad_ref, cos_ref, sin_ref, open_ref, *refs):
    mixed_ref, out_ref, key_ref, value_ref = refs[-4:]
    length = qkv_ref.shape[0]
    wide = 2 * half
    lane = lax.broadcasted_iota(jnp.int32, (length, wide), 1)
    turned = ROT // 2
    leading = (lane % half) < turned
    cosine, sine = cos_ref[...], sin_ref[...]
    scale = half ** (-0.5)

    def turn(x, s):
        other = jnp.where(leading, pltpu.roll(x, wide - turned, 1), pltpu.roll(x, turned, 1))
        return x * cosine + other * s

    query = turn(qkv_ref[:, :wide], sine).astype(BF)
    key = turn(qkv_ref[:, wide : 2 * wide], sine).astype(BF)
    value = qkv_ref[:, 2 * wide :].astype(BF)
    query = (query.astype(F32) * scale).astype(BF)
    grad = grad_ref[...]
    key_t = key.astype(F32).T.astype(BF)
    value_t = value.astype(F32).T.astype(BF)
    key_ref[...] = jnp.zeros_like(key_ref)
    value_ref[...] = jnp.zeros_like(value_ref)
    zero = jnp.zeros((), BF)
    for begin in range(0, length, rows):
        end = begin + rows
        cut = slice(begin, end)
        k_pos = lax.broadcasted_iota(jnp.int32, (end, rows), 0)
        q_pos = lax.broadcasted_iota(jnp.int32, (end, rows), 1) + begin
        allowed = (k_pos <= q_pos) & (k_pos >= open_ref[:, cut])
        side = lane[:rows] < half
        mixed_t, query_t = [], []
        for head in range(2):
            here = side if head == 0 else ~side
            q_rows = jnp.where(here, query[cut], zero)
            g_rows = jnp.where(here, grad[cut], zero)
            scores = jnp.where(allowed, mm(key[:end], q_rows, 1, 1), -1000000000.0)
            expo = jnp.exp(scores - jnp.max(scores, axis=0, keepdims=True))
            probs = expo * (1.0 / jnp.sum(expo, axis=0, keepdims=True))
            low = probs.astype(BF)
            own = slice(head * half, (head + 1) * half)
            mixed_t.append(mm(value_t[own, :end], low))
            grad_probs = mm(value[:end], g_rows, 1, 1)
            dots = jnp.sum(probs * grad_probs, axis=0, keepdims=True)
            grad_scores = (probs * (grad_probs - dots)).astype(BF)
            query_t.append(mm(key_t[own, :end], grad_scores))
            key_ref[:end] += mm(grad_scores, q_rows)
            value_ref[:end] += mm(low, g_rows)
        mixed_ref[cut] = jnp.concatenate(mixed_t, axis=0).T.astype(BF)
        q_grad = jnp.concatenate(query_t, axis=0).T * scale
        lead = leading[:rows]
        other = jnp.where(
            lead, pltpu.roll(q_grad, wide - turned, 1), pltpu.roll(q_grad, turned, 1)
        )
        out_ref[cut, :wide] = (q_grad * cosine[cut] - other * sine[cut]).astype(BF)
    out_ref[:, wide : 2 * wide] = turn(key_ref[...], -sine).astype(BF)
    out_ref[:, 2 * wide :] = value_ref[...].astype(BF)


def attention(qkv, grad, cosine, sine, opening, begin, steps, before=(), after=()):
    length = qkv.shape[0]
    wide = 2 * HEAD_DIM
    pairs = grad.shape[1] // wide

    def whole(array):
        return pl.BlockSpec(array.shape, lambda p: (0, 0))

    narrow = pl.BlockSpec((length, wide), lambda p: (0, begin + p))
    three = pl.BlockSpec((length, 3 * wide), lambda p: (0, begin + p))
    return pl.pallas_call(
        functools.partial(attention_kernel, min(256, length), HEAD_DIM),
        grid=(steps,),
        in_specs=[three, narrow, whole(cosine), whole(sine), whole(opening)]
        + unread(before)
        + unread(after),
        out_specs=[narrow, three],
        out_shape=[
            jax.ShapeDtypeStruct((length, pairs * wide), BF),
            jax.ShapeDtypeStruct((length, pairs * 3 * wide), BF),
        ],
        input_output_aliases={5 + i: i for i in range(len(before))},
        scratch_shapes=[pltpu.VMEM((length, wide), F32), pltpu.VMEM((length, wide), F32)],
        compiler_params=params(),
        cost_estimate=cost(
            24 * length * length * wide * steps,
            24 * length * wide * steps,
            length * length * steps,
        ),
    )(qkv, grad, cosine, sine, opening, *before, *after)


def norm_kernel(in_ref, gain_ref, shift_ref, out_ref, mean_ref, std_ref):
    value = in_ref[...].astype(F32)
    mean = jnp.mean(value, axis=-1, keepdims=True)
    centred = value - mean
    std = lax.rsqrt(jnp.mean(centred * centred, axis=-1, keepdims=True) + EPS)
    out_ref[...] = (centred * std * gain_ref[...] + shift_ref[...]).astype(BF)
    mean_ref[...] = mean
    std_ref[...] = std


def layer_norm(rows_in, gain, shift):
    rows, columns = rows_in.shape
    cut = min(256, rows)
    block = pl.BlockSpec((cut, columns), lambda i: (i, 0))
    vector = pl.BlockSpec((1, columns), lambda i: (0, 0))
    narrow = pl.BlockSpec((cut, 1), lambda i: (i, 0))
    return pl.pallas_call(
        norm_kernel,
        grid=(rows // cut,),
        in_specs=[block, vector, vector],
        out_specs=[block, narrow, narrow],
        out_shape=[
            jax.ShapeDtypeStruct((rows, columns), BF),
            jax.ShapeDtypeStruct((rows, 1), F32),
            jax.ShapeDtypeStruct((rows, 1), F32),
        ],
        compiler_params=params(),
        cost_estimate=cost(10 * rows * columns, 4 * rows * columns),
    )(rows_in, gain[None], shift[None])


def mixed_kernel(cut, high, left_ref, both_ref, *refs):
    weight_ref, out_ref = refs[-2:]
    wide = both_ref.shape[1]
    for i in range(both_ref.shape[0] // high):
        rows = slice(i // cut * high, (i // cut + 1) * high)
        columns = slice(i % cut * wide, (i % cut + 1) * wide)
        weight_ref[rows, columns] = both_ref[i * high : (i + 1) * high, :]
    out_ref[...] = mm(left_ref[...], weight_ref[...], 1, 1).astype(BF)


def mixed_gradient(left, both, begin, cut, high, after=()):
    rows, depth = left.shape
    wide = depth // cut
    weight = (both.shape[0] // cut, depth)

    def whole(shape):
        return pl.BlockSpec(shape, lambda i: (0, 0))

    return pl.pallas_call(
        functools.partial(mixed_kernel, cut, high),
        grid=(1,),
        in_specs=[
            whole(left.shape),
            pl.BlockSpec((both.shape[0], wide), lambda i: (0, begin // wide)),
        ]
        + unread(after),
        out_specs=[whole(weight), whole((rows, weight[0]))],
        out_shape=[
            jax.ShapeDtypeStruct(weight, BF),
            jax.ShapeDtypeStruct((rows, weight[0]), BF),
        ],
        compiler_params=params(),
        cost_estimate=cost(2 * rows * depth * weight[0], 4 * rows * depth),
    )(left, both, *after)


def hidden_kernel(left_ref, right_ref, bias_ref, active_ref, slope_ref):
    value = mm(left_ref[...], right_ref[...]) + bias_ref[...]
    square = value * value
    scaled = 0.7978845608028654 * value
    bend = 0.044715 * square
    tanh = jnp.tanh(scaled * (1.0 + bend))
    half = 0.5 * (1.0 + tanh)
    active_ref[...] = (value * half).astype(BF)
    slope = half + 0.5 * (1.0 - tanh * tanh) * scaled * (1.0 + 3.0 * bend)
    slope_ref[...] = slope.astype(BF)


def hidden_layer(left, right, bias):
    rows, depth = left.shape
    columns = bias.shape[0]
    cut = min(512, columns)
    block = pl.BlockSpec((rows, cut), lambda j: (0, j))
    return pl.pallas_call(
        hidden_kernel,
        grid=(columns // cut,),
        in_specs=[
            pl.BlockSpec((rows, depth), lambda j: (0, 0)),
            pl.BlockSpec((depth, cut), lambda j: (0, j)),
            pl.BlockSpec((1, cut), lambda j: (0, j)),
        ],
        out_specs=[block, block],
        out_shape=[jax.ShapeDtypeStruct((rows, columns), BF)] * 2,
        compiler_params=params(),
        cost_estimate=cost(2 * rows * depth * columns, 4 * rows * (depth + columns), rows * columns),
    )(left, right, bias[None])


def term_kernel(adds, index_ref, left_ref, right_ref, *refs):
    value = mm(left_ref[...], right_ref[...], 0, 0)
    if adds:
        value = value + refs[0][0].astype(F32)
    refs[-1][0] = value.astype(BF)


def block_terms(left, right, width, index, add=None, after=()):
    rows, columns = right.shape
    count = len(index)
    if width % 128:
        blocks = [lax.dynamic_slice_in_dim(left, i * width, width, 1) for i in index]
        value = jnp.stack([mm(block, right, 0, 0) for block in blocks])
        return (value if add is None else value + add.astype(F32)).astype(BF)
    index = jnp.stack([jnp.asarray(i, jnp.int32) for i in index])
    adds = [] if add is None else [add]
    out = pl.BlockSpec((1, width, columns), lambda r, index: (r, 0, 0))
    return pl.pallas_call(
        functools.partial(term_kernel, len(adds)),
        grid_spec=pltpu.PrefetchScalarGridSpec(
            num_scalar_prefetch=1,
            grid=(count,),
            in_specs=[
                pl.BlockSpec((rows, width), lambda r, index: (0, index[r])),
                pl.BlockSpec((rows, columns), lambda r, index: (0, 0)),
            ]
            + [out] * len(adds)
            + unread(after),
            out_specs=out,
        ),
        out_shape=jax.ShapeDtypeStruct((count, width, columns), BF),
        compiler_params=params(),
        cost_estimate=cost(2 * rows * width * count * columns, 4 * rows * columns),
    )(index, left, right, *adds, *after)


def rows_kernel(left_ref, right_ref, *refs):
    refs[-1][...] = mm(left_ref[...], right_ref[...], 0, 0).astype(BF)


def row_terms(left, right, width, total, place, before=()):
    rows, columns = right.shape
    count = left.shape[1] // width
    return pl.pallas_call(
        rows_kernel,
        grid=(count,),
        in_specs=[
            pl.BlockSpec((rows, width), lambda r: (0, r)),
            pl.BlockSpec((rows, columns), lambda r: (0, 0)),
        ]
        + unread(before),
        out_specs=pl.BlockSpec((width, columns), lambda r: (r, place)),
        out_shape=jax.ShapeDtypeStruct((left.shape[1], total), BF),
        input_output_aliases={2 + i: i for i in range(len(before))},
        compiler_params=params(),
        cost_estimate=cost(2 * rows * width * count * columns, 4 * rows * columns),
    )(left, right, *before)


def two_terms_kernel(cut, adds, index_ref, left_ref, right_ref, beside_ref, *refs):
    out_ref = refs[-1]
    columns = right_ref.shape[1]
    value = mm(left_ref[...], right_ref[...], 0, 0)
    if adds:
        value = value + refs[0][0, :, :columns].astype(F32)
    out_ref[0, :, :columns] = value.astype(BF)
    high = beside_ref.shape[1]
    wide = beside_ref.shape[2] // cut
    for i in range(cut):
        part = slice(i * high, (i + 1) * high)
        value = beside_ref[0, :, i * wide : (i + 1) * wide]
        if adds:
            value = (value.astype(F32) + refs[0][0, part, columns:].astype(F32)).astype(BF)
        out_ref[0, part, columns:] = value


def two_terms(left, right, width, beside, cut, index, add=None, after=()):
    rows, columns = right.shape
    count = len(index)
    extra = beside.shape[2] // cut
    index = jnp.stack([jnp.asarray(i, jnp.int32) for i in index])
    adds = [] if add is None else [add]
    out = pl.BlockSpec((1, width, columns + extra), lambda r, index: (r, 0, 0))
    return pl.pallas_call(
        functools.partial(two_terms_kernel, cut, len(adds)),
        grid_spec=pltpu.PrefetchScalarGridSpec(
            num_scalar_prefetch=1,
            grid=(count,),
            in_specs=[
                pl.BlockSpec((rows, width), lambda r, index: (0, index[r])),
                pl.BlockSpec((rows, columns), lambda r, index: (0, 0)),
                pl.BlockSpec((1,) + beside.shape[1:], lambda r, index: (index[r], 0, 0)),
            ]
            + [out] * len(adds)
            + unread(after),
            out_specs=out,
        ),
        out_shape=jax.ShapeDtypeStruct((count, width, columns + extra), BF),
        compiler_params=params(),
        cost_estimate=cost(2 * rows * width * count * columns, 4 * rows * columns),
    )(index, left, right, beside, *adds, *after)


def product_kernel(left_ref, right_ref, bias_ref, *refs):
    refs[-1][...] = mm(left_ref[...], right_ref[...]) + bias_ref[...]


def product(left, right, bias, after=()):
    rows, depth = left.shape
    columns = bias.shape[0]
    cut = 512 if columns % 512 == 0 else 256
    return pl.pallas_call(
        product_kernel,
        grid=(columns // cut,),
        in_specs=[
            pl.BlockSpec((rows, depth), lambda j: (0, 0)),
            pl.BlockSpec((depth, cut), lambda j: (0, j)),
            pl.BlockSpec((1, cut), lambda j: (0, j)),
        ]
        + unread(after),
        out_specs=pl.BlockSpec((rows, cut), lambda j: (0, j)),
        out_shape=jax.ShapeDtypeStruct((rows, columns), F32),
        compiler_params=params(),
        cost_estimate=cost(2 * rows * depth * columns, 4 * rows * (depth + columns)),
    )(left, right, bias[None], *after)


def slope_kernel(left_ref, right_ref, slope_ref, *refs):
    value = mm(left_ref[...], right_ref[...], 1, 1) * slope_ref[...].astype(F32)
    refs[-1][...] = value.astype(BF)


def times_slope(left, right, begin, slope, after=()):
    rows, depth = left.shape
    columns = right.shape[0]
    cut = min(512, columns)
    block = pl.BlockSpec((rows, cut), lambda j: (0, j))
    return pl.pallas_call(
        slope_kernel,
        grid=(columns // cut,),
        in_specs=[
            pl.BlockSpec((rows, depth), lambda j: (0, 0)),
            pl.BlockSpec((cut, depth), lambda j: (j, begin // depth)),
            block,
        ]
        + unread(after),
        out_specs=block,
        out_shape=jax.ShapeDtypeStruct(slope.shape, BF),
        compiler_params=params(),
        cost_estimate=cost(2 * rows * depth * columns, 6 * rows * depth),
    )(left, right, slope, *after)


def output_kernel(left_ref, right_ref, second_ref, weight_ref, *refs):
    value = mm(left_ref[...], right_ref[...]) + mm(second_ref[...], weight_ref[...])
    refs[-1][...] = value.astype(BF)


def output_terms(left, right, begin, second, weight, after=()):
    rows, depth = left.shape
    columns = weight.shape[1]
    cut = min(512, columns)
    return pl.pallas_call(
        output_kernel,
        grid=(columns // cut,),
        in_specs=[
            pl.BlockSpec((rows, depth), lambda j: (0, 0)),
            pl.BlockSpec((depth, cut), lambda j: (0, begin // cut + j)),
            pl.BlockSpec(second.shape, lambda j: (0, 0)),
            pl.BlockSpec((second.shape[1], cut), lambda j: (0, j)),
        ]
        + unread(after),
        out_specs=pl.BlockSpec((rows, cut), lambda j: (0, j)),
        out_shape=jax.ShapeDtypeStruct((rows, columns), BF),
        compiler_params=params(),
        cost_estimate=cost(2 * rows * (depth + second.shape[1]) * columns, 6 * rows * depth),
    )(left, right, second, weight, *after)


def normed_kernel(one_ref, first_ref, two_ref, second_ref, in_ref, mean_ref, std_ref, *refs):
    out_ref, gain_ref, shift_ref = refs[-3:]
    value = mm(one_ref[...], first_ref[...], 1, 1) + mm(two_ref[...], second_ref[...], 1, 1)
    out_ref[...] = value.astype(BF)
    normal_hat = (in_ref[...].astype(F32) - mean_ref[...]) * std_ref[...]
    gain_ref[...] = jnp.sum(value * normal_hat, axis=0, keepdims=True)
    shift_ref[...] = jnp.sum(value, axis=0, keepdims=True)


def normed_terms(one, first, two, second, rows_in, mean, std, after=()):
    rows = one.shape[0]
    columns = first.shape[0]
    cut = min(512, columns)
    vector = pl.BlockSpec((1, cut), lambda j: (0, j))

    def whole(array):
        return pl.BlockSpec(array.shape, lambda j: (0, 0))

    return pl.pallas_call(
        normed_kernel,
        grid=(columns // cut,),
        in_specs=[
            whole(one),
            pl.BlockSpec((cut, one.shape[1]), lambda j: (j, 0)),
            whole(two),
            pl.BlockSpec((cut, two.shape[1]), lambda j: (j, 0)),
            pl.BlockSpec((rows, cut), lambda j: (0, j)),
            whole(mean),
            whole(std),
        ]
        + unread(after),
        out_specs=[pl.BlockSpec((rows, cut), lambda j: (0, j)), vector, vector],
        out_shape=[
            jax.ShapeDtypeStruct((rows, columns), BF),
            jax.ShapeDtypeStruct((1, columns), F32),
            jax.ShapeDtypeStruct((1, columns), F32),
        ],
        compiler_params=params(),
        cost_estimate=cost(2 * rows * columns * (one.shape[1] + two.shape[1]), 8 * rows * columns),
    )(one, first, two, second, rows_in, mean, std, *after)


def spread_kernel(width, in_ref, out_ref):
    for s in range(in_ref.shape[0]):
        out_ref[:, s * width : (s + 1) * width] = in_ref[s].astype(F32)


def spread_columns(pieces, width):
    count, rows, columns = pieces.shape
    return pl.pallas_call(
        functools.partial(spread_kernel, width),
        grid=(columns // width,),
        in_specs=[pl.BlockSpec((count, rows, width), lambda i: (0, 0, i))],
        out_specs=pl.BlockSpec((rows, width * count), lambda i: (0, i)),
        out_shape=jax.ShapeDtypeStruct((rows, columns * count), F32),
        compiler_params=params(),
        cost_estimate=cost(0, 6 * rows * columns * count),
    )(pieces)


def heads_kernel(half, in_ref, out_ref):
    parts = []
    for head in range(2):
        for s in range(in_ref.shape[0]):
            for part in range(3):
                start = (2 * part + head) * half
                parts.append(in_ref[s, :, start : start + half].astype(F32))
    for i in range(0, len(parts), 2):
        out_ref[:, i * half : (i + 2) * half] = jnp.concatenate(parts[i : i + 2], axis=1)


def spread_heads(pieces, pairs):
    count, rows, unused = pieces.shape
    width = 6 * HEAD_DIM
    return pl.pallas_call(
        functools.partial(heads_kernel, HEAD_DIM),
        grid=(pairs,),
        in_specs=[pl.BlockSpec((count, rows, width), lambda i: (0, 0, i))],
        out_specs=pl.BlockSpec((rows, width * count), lambda i: (0, i)),
        out_shape=jax.ShapeDtypeStruct((rows, pairs * width * count), F32),
        compiler_params=params(),
        cost_estimate=cost(0, 6 * rows * pairs * width * count),
    )(pieces)


def by_pairs(array, heads):
    lead = array.shape[:-1]
    array = array.reshape(lead + (heads // 2, 2, 3, HEAD_DIM))
    return jnp.swapaxes(array, -3, -2).reshape(lead + (heads * 3 * HEAD_DIM,))


def by_heads(array, heads):
    lead = array.shape[:-1]
    array = array.reshape(lead + (heads // 2, 3, 2, HEAD_DIM))
    return jnp.swapaxes(array, -3, -2).reshape(lead + (heads * 3 * HEAD_DIM,))


def per_device(
    inputs,
    doc_starts,
    ln_gain,
    ln_bias,
    w_qkv,
    b_qkv,
    w_out,
    b_out,
    w_fc1,
    b_fc1,
    w_fc2,
    b_fc2,
    cotangent,
):
    seqs, shards = lax.axis_size("seq"), lax.axis_size("fsdp")
    me = lax.axis_index("seq")
    chips, chip, core = fsdp_place()
    tok, width = inputs.shape[1:]
    length = tok * seqs
    rows_here = w_qkv.shape[0]
    heads = HEADS // seqs
    head_cols = heads * HEAD_DIM
    shard_heads = w_out.shape[0] // HEAD_DIM
    strided = shard_heads % seqs == 0
    each = shard_heads // seqs
    unit = w_fc2.shape[0] // seqs
    hidden_cols = unit * shards
    order = [2 * ((chip + r) % chips) + (core ^ h) for h in (0, 1) for r in range(chips)]

    fc1_here = jnp.concatenate(
        [
            lax.dynamic_slice_in_dim(w_fc1, (i * seqs + me) * unit, unit, 1)
            for i in range(shards)
        ],
        axis=1,
    )
    fc2_here = pick(w_fc2.reshape(seqs, unit, width), me)
    if strided:
        qkv_here = pick(w_qkv.reshape(rows_here, shards, seqs, each * 3 * HEAD_DIM), me, 2)
    else:
        qkv_here = pick(w_qkv.reshape(rows_here, seqs, heads * 3 * HEAD_DIM), me, 1)
    qkv_here = by_pairs(qkv_here.reshape(rows_here, 3 * head_cols), heads)
    out_cut = rows_here // (each * HEAD_DIM) if strided else 1
    if strided:
        out_here = pick(w_out.reshape(seqs, each * HEAD_DIM, width), me)
        out_here = out_here.reshape(each * HEAD_DIM, out_cut, width // out_cut)
        out_here = jnp.swapaxes(out_here, 0, 1).reshape(rows_here, width // out_cut)
        qkv_here = jnp.concatenate([qkv_here, out_here], axis=1)

    sizes = [v.shape[0] for v in (ln_gain, ln_bias, b_out, b_fc2, b_qkv, b_fc1)]
    small = jnp.concatenate([ln_gain, ln_bias, b_out, b_fc2, b_qkv, b_fc1])[None]
    small = lax.all_gather(small, "fsdp", axis=0, tiled=True).astype(F32)
    cuts = [sum(sizes[:i]) for i in range(len(sizes) + 1)]
    gain, shift, bias_out, bias_fc2, bias_qkv, bias_fc1 = [
        small[:, a:b].reshape(-1) for a, b in zip(cuts[:-1], cuts[1:])
    ]
    bias_fc1 = pick(bias_fc1.reshape(shards, seqs, unit), me, 1).reshape(hidden_cols)
    if strided:
        bias_qkv = pick(bias_qkv.reshape(shards, seqs, each * 3 * HEAD_DIM), me, 1)
    else:
        bias_qkv = pick(bias_qkv.reshape(seqs, heads * 3 * HEAD_DIM), me)
    bias_qkv = by_pairs(bias_qkv.reshape(3 * head_cols), heads)

    joined = rows_here == unit and hidden_cols == width and unit % 128 == 0
    if joined:
        fc1 = fc2 = fsdp_gather(jnp.concatenate([fc1_here, fc2_here], axis=1))
        begin = hidden_cols
    else:
        fc1, fc2, begin = fsdp_gather(fc1_here), fsdp_gather(fc2_here), 0
    rows_all, grad_rows = seq_gather_two(inputs[0], cotangent[0])
    rows_all, grad_rows = rows_all.reshape(length, width), grad_rows.reshape(length, width)

    starts_row = doc_starts[0]
    pos = jnp.arange(length, dtype=jnp.int32)
    before = starts_row[None, :] <= pos[:, None]
    opening = jnp.max(jnp.where(before, starts_row[None, :], 0), axis=1)
    rates = 10000.0 ** (-2.0 * jnp.arange(ROT // 2, dtype=F32) / ROT)
    angle = (pos - opening).astype(F32)[:, None] * rates[None, :]
    cosine, sine = jnp.cos(angle), jnp.sin(angle)
    rest = jnp.ones((length, HEAD_DIM - ROT), F32)
    cosine = jnp.concatenate([cosine, cosine, rest] * 2, axis=1)
    sine = jnp.concatenate([-sine, sine, 0.0 * rest] * 2, axis=1)

    normed, mean, inv_std = layer_norm(rows_all, behind(gain, grad_rows), shift)
    both = fsdp_gather(behind(qkv_here, normed))
    mine, others = order[:chips], order[chips:]

    active, slope = hidden_layer(normed, fc1, bias_fc1)
    if joined:
        terms = row_terms(active, grad_rows, unit, 2 * width, 0)
        grad_hidden = times_slope(grad_rows, fc2, begin, slope, [terms])
        terms = row_terms(normed, grad_hidden, rows_here, 2 * width, 1, [terms])
        sums = fsdp_sum(terms)
        part_fc2, part_fc1 = sums[:, :width], sums[:, width:]
    else:
        part_fc2 = fsdp_sum(mm(active, grad_rows, 0, 0).astype(BF))
        grad_hidden = times_slope(grad_rows, fc2, begin, slope)
        terms = mm(normed, grad_hidden, 0, 0).astype(BF)
        part_fc1 = fsdp_sum(terms)

    if strided:
        high = each * HEAD_DIM
        out_w, grad_mixed = mixed_gradient(grad_rows, both, 3 * head_cols, out_cut, high, [terms])
    else:
        out_w = pick(fsdp_gather(w_out).reshape(seqs, head_cols, width), me)
        grad_mixed = mm(grad_rows, out_w, 1, 1).astype(BF)
    qkv = product(normed, both, bias_qkv, [grad_mixed])
    tables = (cosine, sine, opening[None])
    mixed, grad_qkv = attention(qkv, grad_mixed, *tables, 0, heads // 2)
    out_grad = mm(mixed, grad_rows, 0, 0).astype(BF)
    if strided:
        out_grad = out_grad.reshape(shards, each * HEAD_DIM, width)
        all_qkv = two_terms(normed, grad_qkv, rows_here, out_grad, out_cut, list(range(shards)))
        all_qkv = all_qkv.reshape(width, -1)
    else:
        spread = put(jnp.zeros((seqs, head_cols, width), BF), out_grad, me)
        part_out = fsdp_sum(spread.reshape(seqs * head_cols, width))
        all_qkv = mm(normed, grad_qkv, 0, 0).astype(BF)
    part_qkv = fsdp_sum(all_qkv)
    partial = output_terms(active, fc2, begin, mixed, out_w, [all_qkv])
    result = seq_sum(partial.reshape(seqs, tok, width))
    grad_partial, sum_gain, sum_shift = normed_terms(
        grad_qkv, both, grad_hidden, fc1, rows_all, mean, inv_std, [partial]
    )
    grad_normed = seq_sum(grad_partial.reshape(seqs, tok, width))
    part_fc2 = behind(part_fc2, result)
    if joined:
        whole_fc2, whole_fc1 = seq_gather_two(part_fc2, part_fc1)
    else:
        whole_fc2, whole_fc1 = seq_all(part_fc2), seq_all(part_fc1)
    whole_qkv = seq_all(behind(behind(part_qkv, grad_normed), whole_fc1))
    output = (inputs[0].astype(F32) + result + (bias_out + bias_fc2)).astype(BF)[None]
    sum_gain, sum_shift = sum_gain[0], sum_shift[0]
    own_std = pick(inv_std.reshape(seqs, tok, 1), me)
    own_hat = (inputs[0].astype(F32) - pick(mean.reshape(seqs, tok, 1), me)) * own_std
    scaled = grad_normed * gain
    grad_in = own_std * (
        scaled
        - jnp.mean(scaled, axis=-1, keepdims=True)
        - own_hat * jnp.mean(scaled * own_hat, axis=-1, keepdims=True)
    )
    grad_in = cotangent[0].astype(F32) + grad_in

    sum_bfc1 = jnp.sum(grad_hidden.astype(F32), axis=0).reshape(shards, unit)
    sum_bfc1 = put(jnp.zeros((shards, seqs, unit), F32), sum_bfc1, me, 1)
    sum_bqkv = by_heads(jnp.sum(grad_qkv.astype(F32), axis=0), heads)
    if strided:
        sum_bqkv = sum_bqkv.reshape(shards, each * 3 * HEAD_DIM)
        sum_bqkv = put(jnp.zeros((shards, seqs, each * 3 * HEAD_DIM), F32), sum_bqkv, me, 1)
    else:
        sum_bqkv = put(jnp.zeros((seqs, heads * 3 * HEAD_DIM), F32), sum_bqkv, me)
    sum_out = jnp.sum(cotangent[0].astype(F32), axis=0)
    vectors = jnp.concatenate(
        [v.reshape(shards, -1) for v in (sum_gain, sum_shift, sum_out, sum_bqkv, sum_bfc1)], axis=1
    )
    vectors = vectors[:, None]
    vectors = LineSum(
        jnp.stack([pick(vectors, i) for i in others]),
        lambda got: jnp.stack([pick(vectors, i) for i in mine]) + got,
    ).total
    vectors = jnp.sum(seq_gather(vectors), axis=(0, 1))
    ends = [sizes[0], sizes[1], sizes[2], sizes[4], sizes[5]]
    ends = [sum(ends[:i]) for i in range(len(ends) + 1)]
    total_gain, total_shift, total_bout, total_bqkv, total_bfc1 = [
        vectors[a:b] for a, b in zip(ends[:-1], ends[1:])
    ]

    total_wfc2 = whole_fc2.astype(F32).reshape(seqs * unit, width)
    if unit % 128 == 0:
        total_wfc1 = spread_columns(whole_fc1, unit)
    else:
        total_wfc1 = whole_fc1.astype(F32).reshape(seqs, rows_here, shards, unit)
        total_wfc1 = total_wfc1.transpose(1, 2, 0, 3).reshape(rows_here, -1)
    if strided and each == 1:
        total_wqkv = spread_heads(whole_qkv, heads // 2)
    else:
        total_wqkv = by_heads(whole_qkv[:, :, : 3 * head_cols].astype(F32), heads)
        if strided:
            total_wqkv = total_wqkv.reshape(seqs, rows_here, shards, each * 3 * HEAD_DIM)
            total_wqkv = total_wqkv.transpose(1, 2, 0, 3).reshape(rows_here, -1)
        else:
            total_wqkv = total_wqkv.transpose(1, 0, 2).reshape(rows_here, -1)
    if strided:
        total_wout = whole_qkv[:, :, 3 * head_cols :].astype(F32)
        total_wout = total_wout.reshape(seqs, out_cut, each * HEAD_DIM, width // out_cut)
        total_wout = jnp.swapaxes(total_wout, 1, 2).reshape(-1, width)
    else:
        total_wout = jnp.sum(seq_all(part_out.astype(BF)).astype(F32), axis=0)
    return (
        output,
        grad_in[None],
        total_gain,
        total_shift,
        total_wqkv,
        total_bqkv,
        total_wout,
        total_bout,
        total_wfc1,
        total_bfc1,
        total_wfc2,
        total_bout,
    )


def solution(mesh):
    rows, vector, matrix = P("fsdp", "seq", None), P("fsdp"), P("fsdp", None)
    weights = (vector, vector) + (matrix, vector) * 4
    return jax.shard_map(
        per_device,
        mesh=mesh,
        in_specs=(rows, matrix) + weights + (rows,),
        out_specs=(rows, rows) + weights,
        check_vma=False,
    )
```

```python
import functools

import jax
import jax.numpy as jnp
from jax import lax
from jax.experimental import pallas as pl
from jax.experimental.pallas import tpu as pltpu
from jax.sharding import PartitionSpec as P

HEADS = 32
HEAD_DIM = 64
ROT = 32
EPS = 1e-05
BF = jnp.bfloat16
F32 = jnp.float32
VMEM_BYTES = 56 * 1024 * 1024


def mm(left, right, left_dim=1, right_dim=0):
    return lax.dot_general(
        left, right, (((left_dim,), (right_dim,)), ((), ())), preferred_element_type=F32
    )


def pick(array, index, axis=0):
    return lax.dynamic_index_in_dim(array, index, axis, keepdims=False)


def put(array, piece, index, axis=0):
    return lax.dynamic_update_index_in_dim(array, piece, index, axis)


def behind(array, other):
    first = lax.slice(other, (0,) * other.ndim, (1,) * other.ndim).reshape(())
    return jnp.where(jnp.isnan(first), jnp.zeros((), array.dtype), array)


def unread(arrays):
    return [pl.BlockSpec(memory_space=pl.ANY) for unused in arrays]


def params():
    return pltpu.CompilerParams(vmem_limit_bytes=VMEM_BYTES)


def cost(flops, size, transcendentals=0):
    return pl.CostEstimate(flops=flops, bytes_accessed=size, transcendentals=transcendentals)


def seq_exchange(blocks):
    return lax.all_to_all(blocks, "seq", split_axis=0, concat_axis=0)


def seq_gather(block):
    count = lax.axis_size("seq")
    return seq_exchange(jnp.broadcast_to(block[None], (count,) + block.shape))


def seq_gather_two(first, second):
    me, count = lax.axis_index("seq"), lax.axis_size("seq")
    bits = list(range(count.bit_length() - 1))
    orders = (bits, bits[::-1])
    wholes = [first[None], second[None]]
    for step in bits:
        got = []
        for whole, order in zip(wholes, orders):
            pairs = [(i, i ^ (1 << order[step])) for i in range(count)]
            got.append(lax.ppermute(whole, "seq", pairs))
        for i, order in enumerate(orders):
            low = (me >> order[step]) % 2 == 0
            whole, new = wholes[i], behind(got[i], got[1 - i])
            whole = jnp.where(low, jnp.stack([whole, new]), jnp.stack([new, whole]))
            wholes[i] = whole.reshape((-1,) + first.shape)
    sizes = (2,) * len(bits) + second.shape
    order = bits[::-1] + [len(bits) + i for i in range(second.ndim)]
    return wholes[0], wholes[1].reshape(sizes).transpose(order).reshape(wholes[1].shape)


def seq_all(block):
    return lax.all_gather(block, "seq", axis=0)


def seq_sum_halves(blocks):
    me, count = lax.axis_index("seq"), lax.axis_size("seq")
    bits = list(range(count.bit_length() - 1))
    half = blocks.shape[-1] // 2
    orders = (bits, bits[::-1])
    shape = (2,) * len(bits) + blocks.shape[1:-1] + (half,)
    parts = [blocks[..., :half].reshape(shape), blocks[..., half:].reshape(shape)]
    left = [list(bits[::-1]), list(bits[::-1])]
    for step in bits:
        got = []
        for i, order in enumerate(orders):
            mine, axis = (me >> order[step]) % 2, left[i].index(order[step])
            pairs = [(j, j ^ (1 << order[step])) for j in range(count)]
            got.append(lax.ppermute(pick(parts[i], 1 - mine, axis), "seq", pairs))
        for i, order in enumerate(orders):
            mine, axis = (me >> order[step]) % 2, left[i].index(order[step])
            left[i].remove(order[step])
            total = pick(parts[i], mine, axis).astype(F32) + behind(got[i], got[1 - i]).astype(F32)
            parts[i] = total.astype(blocks.dtype) if left[i] else total
    return jnp.concatenate(parts, axis=-1)


def seq_sum(blocks):
    return jnp.sum(seq_exchange(blocks).astype(F32), axis=0)


def fsdp_place():
    me = lax.axis_index("fsdp")
    return lax.axis_size("fsdp") // 2, me // 2, me % 2


def to_chips(array, moves):
    pairs = [(2 * a + core, 2 * b + core) for a, b in moves for core in (0, 1)]
    return lax.ppermute(array, "fsdp", pairs)


def to_other_core(array):
    count = lax.axis_size("fsdp")
    return lax.ppermute(array, "fsdp", [(i, i ^ 1) for i in range(count)])


def fsdp_gather(block):
    return lax.all_gather(block, "fsdp", axis=0, tiled=True)


def fsdp_sum(parts):
    return lax.psum_scatter(parts, "fsdp", scatter_dimension=0, tiled=True)


class LineSum:
    def __init__(self, other, own_of):
        chips, chip, core = fsdp_place()
        own = own_of(to_other_core(other))
        first = jnp.where(chip == 0, own[chips - 1], own[1])
        got = to_chips(first, [(chips - 1, chips - 2), (0, 1)])
        self.first = first
        self.steps = [own, got]
        total = own[0].astype(F32) + got.astype(F32)
        down, up = got, got
        for step in range(2, chips):
            down = (down.astype(F32) + own[step].astype(F32)).astype(own.dtype)
            up = (up.astype(F32) + own[chips - step].astype(F32)).astype(own.dtype)
            down = to_chips(down, [(a, a - 1) for a in range(chips - step, chips)])
            up = to_chips(up, [(a, a + 1) for a in range(0, step)])
            self.steps += [down, up]
        if chips > 2:
            total = own[0].astype(F32) + down.astype(F32) + up.astype(F32)
        self.total = total


def attention_kernel(rows, half, qkv_ref, grad_ref, cos_ref, sin_ref, open_ref, *refs):
    mixed_ref, out_ref, key_ref, value_ref = refs[-4:]
    length = qkv_ref.shape[0]
    wide = 2 * half
    lane = lax.broadcasted_iota(jnp.int32, (length, wide), 1)
    turned = ROT // 2
    leading = (lane % half) < turned
    cosine, sine = cos_ref[...], sin_ref[...]
    scale = half ** (-0.5)

    def turn(x, s):
        other = jnp.where(leading, pltpu.roll(x, wide - turned, 1), pltpu.roll(x, turned, 1))
        return x * cosine + other * s

    query = turn(qkv_ref[:, :wide], sine).astype(BF)
    key = turn(qkv_ref[:, wide : 2 * wide], sine).astype(BF)
    value = qkv_ref[:, 2 * wide :].astype(BF)
    query = (query.astype(F32) * scale).astype(BF)
    grad = grad_ref[...]
    key_t = key.astype(F32).T.astype(BF)
    value_t = value.astype(F32).T.astype(BF)
    key_ref[...] = jnp.zeros_like(key_ref)
    value_ref[...] = jnp.zeros_like(value_ref)
    zero = jnp.zeros((), BF)
    for begin in range(0, length, rows):
        end = begin + rows
        cut = slice(begin, end)
        k_pos = lax.broadcasted_iota(jnp.int32, (end, rows), 0)
        q_pos = lax.broadcasted_iota(jnp.int32, (end, rows), 1) + begin
        allowed = (k_pos <= q_pos) & (k_pos >= open_ref[:, cut])
        side = lane[:rows] < half
        mixed_t, query_t = [], []
        for head in range(2):
            here = side if head == 0 else ~side
            q_rows = jnp.where(here, query[cut], zero)
            g_rows = jnp.where(here, grad[cut], zero)
            scores = jnp.where(allowed, mm(key[:end], q_rows, 1, 1), -1000000000.0)
            expo = jnp.exp(scores - jnp.max(scores, axis=0, keepdims=True))
            probs = expo * (1.0 / jnp.sum(expo, axis=0, keepdims=True))
            low = probs.astype(BF)
            own = slice(head * half, (head + 1) * half)
            mixed_t.append(mm(value_t[own, :end], low))
            grad_probs = mm(value[:end], g_rows, 1, 1)
            dots = jnp.sum(probs * grad_probs, axis=0, keepdims=True)
            grad_scores = (probs * (grad_probs - dots)).astype(BF)
            query_t.append(mm(key_t[own, :end], grad_scores))
            key_ref[:end] += mm(grad_scores, q_rows)
            value_ref[:end] += mm(low, g_rows)
        mixed_ref[cut] = jnp.concatenate(mixed_t, axis=0).T.astype(BF)
        q_grad = jnp.concatenate(query_t, axis=0).T * scale
        lead = leading[:rows]
        other = jnp.where(
            lead, pltpu.roll(q_grad, wide - turned, 1), pltpu.roll(q_grad, turned, 1)
        )
        out_ref[cut, :wide] = (q_grad * cosine[cut] - other * sine[cut]).astype(BF)
    out_ref[:, wide : 2 * wide] = turn(key_ref[...], -sine).astype(BF)
    out_ref[:, 2 * wide :] = value_ref[...].astype(BF)


def attention(qkv, grad, cosine, sine, opening, begin, steps, before=(), after=()):
    length = qkv.shape[0]
    wide = 2 * HEAD_DIM
    pairs = grad.shape[1] // wide

    def whole(array):
        return pl.BlockSpec(array.shape, lambda p: (0, 0))

    narrow = pl.BlockSpec((length, wide), lambda p: (0, begin + p))
    three = pl.BlockSpec((length, 3 * wide), lambda p: (0, begin + p))
    return pl.pallas_call(
        functools.partial(attention_kernel, min(256, length), HEAD_DIM),
        grid=(steps,),
        in_specs=[three, narrow, whole(cosine), whole(sine), whole(opening)]
        + unread(before)
        + unread(after),
        out_specs=[narrow, three],
        out_shape=[
            jax.ShapeDtypeStruct((length, pairs * wide), BF),
            jax.ShapeDtypeStruct((length, pairs * 3 * wide), BF),
        ],
        input_output_aliases={5 + i: i for i in range(len(before))},
        scratch_shapes=[pltpu.VMEM((length, wide), F32), pltpu.VMEM((length, wide), F32)],
        compiler_params=params(),
        cost_estimate=cost(
            24 * length * length * wide * steps,
            24 * length * wide * steps,
            length * length * steps,
        ),
    )(qkv, grad, cosine, sine, opening, *before, *after)


def pick_kernel(me_ref, *refs):
    *pieces, second_ref, out_ref = refs
    step = pl.program_id(0)
    unit = pieces[0].shape[1]

    @pl.when(step < 2)
    def _():
        for i, piece in enumerate(pieces):
            out_ref[:, i * unit : (i + 1) * unit] = piece[...]

    @pl.when(step >= 2)
    def _():
        out_ref[...] = second_ref[...]


def pick_two(first, second, unit):
    seqs = lax.axis_size("seq")
    rows, columns = first.shape[0], first.shape[1] // seqs
    count = columns // unit // 2
    me = lax.axis_index("seq").astype(jnp.int32).reshape(1)

    def piece(i):
        return pl.BlockSpec(
            (rows, unit), lambda j, me: (0, (jnp.minimum(j, 1) * count + i) * seqs + me[0])
        )

    return pl.pallas_call(
        pick_kernel,
        grid_spec=pltpu.PrefetchScalarGridSpec(
            num_scalar_prefetch=1,
            grid=(4,),
            in_specs=[piece(i) for i in range(count)]
            + [
                pl.BlockSpec(
                    (unit, columns // 2), lambda j, me: (me[0], jnp.maximum(j - 2, 0))
                )
            ],
            out_specs=pl.BlockSpec((rows, columns // 2), lambda j, me: (0, j)),
        ),
        out_shape=jax.ShapeDtypeStruct((rows, 2 * columns), BF),
        compiler_params=params(),
        cost_estimate=cost(0, 8 * rows * columns),
    )(me, *([first] * count), second)


def norm_kernel(in_ref, gain_ref, shift_ref, out_ref, mean_ref, std_ref):
    value = in_ref[...].astype(F32)
    mean = jnp.mean(value, axis=-1, keepdims=True)
    centred = value - mean
    std = lax.rsqrt(jnp.mean(centred * centred, axis=-1, keepdims=True) + EPS)
    out_ref[...] = (centred * std * gain_ref[...] + shift_ref[...]).astype(BF)
    mean_ref[...] = mean
    std_ref[...] = std


def layer_norm(rows_in, gain, shift):
    rows, columns = rows_in.shape
    cut = min(256, rows)
    block = pl.BlockSpec((cut, columns), lambda i: (i, 0))
    vector = pl.BlockSpec((1, columns), lambda i: (0, 0))
    narrow = pl.BlockSpec((cut, 1), lambda i: (i, 0))
    return pl.pallas_call(
        norm_kernel,
        grid=(rows // cut,),
        in_specs=[block, vector, vector],
        out_specs=[block, narrow, narrow],
        out_shape=[
            jax.ShapeDtypeStruct((rows, columns), BF),
            jax.ShapeDtypeStruct((rows, 1), F32),
            jax.ShapeDtypeStruct((rows, 1), F32),
        ],
        compiler_params=params(),
        cost_estimate=cost(10 * rows * columns, 4 * rows * columns),
    )(rows_in, gain[None], shift[None])


def mixed_kernel(cut, high, left_ref, both_ref, *refs):
    weight_ref, out_ref = refs[-2:]
    wide = both_ref.shape[1]
    for i in range(both_ref.shape[0] // high):
        rows = slice(i // cut * high, (i // cut + 1) * high)
        columns = slice(i % cut * wide, (i % cut + 1) * wide)
        weight_ref[rows, columns] = both_ref[i * high : (i + 1) * high, :]
    out_ref[...] = mm(left_ref[...], weight_ref[...], 1, 1).astype(BF)


def mixed_gradient(left, both, begin, cut, high, after=()):
    rows, depth = left.shape
    wide = depth // cut
    weight = (both.shape[0] // cut, depth)

    def whole(shape):
        return pl.BlockSpec(shape, lambda i: (0, 0))

    return pl.pallas_call(
        functools.partial(mixed_kernel, cut, high),
        grid=(1,),
        in_specs=[
            whole(left.shape),
            pl.BlockSpec((both.shape[0], wide), lambda i: (0, begin // wide)),
        ]
        + unread(after),
        out_specs=[whole(weight), whole((rows, weight[0]))],
        out_shape=[
            jax.ShapeDtypeStruct(weight, BF),
            jax.ShapeDtypeStruct((rows, weight[0]), BF),
        ],
        compiler_params=params(),
        cost_estimate=cost(2 * rows * depth * weight[0], 4 * rows * depth),
    )(left, both, *after)


def hidden_kernel(left_ref, right_ref, bias_ref, active_ref, slope_ref):
    value = mm(left_ref[...], right_ref[...]) + bias_ref[...]
    square = value * value
    scaled = 0.7978845608028654 * value
    bend = 0.044715 * square
    tanh = jnp.tanh(scaled * (1.0 + bend))
    half = 0.5 * (1.0 + tanh)
    active_ref[...] = (value * half).astype(BF)
    slope = half + 0.5 * (1.0 - tanh * tanh) * scaled * (1.0 + 3.0 * bend)
    slope_ref[...] = slope.astype(BF)


def hidden_layer(left, right, bias):
    rows, depth = left.shape
    columns = bias.shape[0]
    cut = min(512, columns)
    block = pl.BlockSpec((rows, cut), lambda j: (0, j))
    return pl.pallas_call(
        hidden_kernel,
        grid=(columns // cut,),
        in_specs=[
            pl.BlockSpec((rows, depth), lambda j: (0, 0)),
            pl.BlockSpec((depth, cut), lambda j: (0, j)),
            pl.BlockSpec((1, cut), lambda j: (0, j)),
        ],
        out_specs=[block, block],
        out_shape=[jax.ShapeDtypeStruct((rows, columns), BF)] * 2,
        compiler_params=params(),
        cost_estimate=cost(2 * rows * depth * columns, 4 * rows * (depth + columns), rows * columns),
    )(left, right, bias[None])


def term_kernel(adds, index_ref, left_ref, right_ref, *refs):
    value = mm(left_ref[...], right_ref[...], 0, 0)
    if adds:
        value = value + refs[0][0].astype(F32)
    refs[-1][0] = value.astype(BF)


def block_terms(left, right, width, index, add=None, after=()):
    rows, columns = right.shape
    count = len(index)
    if width % 128:
        blocks = [lax.dynamic_slice_in_dim(left, i * width, width, 1) for i in index]
        value = jnp.stack([mm(block, right, 0, 0) for block in blocks])
        return (value if add is None else value + add.astype(F32)).astype(BF)
    index = jnp.stack([jnp.asarray(i, jnp.int32) for i in index])
    adds = [] if add is None else [add]
    out = pl.BlockSpec((1, width, columns), lambda r, index: (r, 0, 0))
    return pl.pallas_call(
        functools.partial(term_kernel, len(adds)),
        grid_spec=pltpu.PrefetchScalarGridSpec(
            num_scalar_prefetch=1,
            grid=(count,),
            in_specs=[
                pl.BlockSpec((rows, width), lambda r, index: (0, index[r])),
                pl.BlockSpec((rows, columns), lambda r, index: (0, 0)),
            ]
            + [out] * len(adds)
            + unread(after),
            out_specs=out,
        ),
        out_shape=jax.ShapeDtypeStruct((count, width, columns), BF),
        compiler_params=params(),
        cost_estimate=cost(2 * rows * width * count * columns, 4 * rows * columns),
    )(index, left, right, *adds, *after)


def rows_kernel(left_ref, right_ref, *refs):
    refs[-1][...] = mm(left_ref[...], right_ref[...], 0, 0).astype(BF)


def row_terms(left, right, width, total, place, before=()):
    rows, columns = right.shape
    count = left.shape[1] // width
    return pl.pallas_call(
        rows_kernel,
        grid=(count,),
        in_specs=[
            pl.BlockSpec((rows, width), lambda r: (0, r)),
            pl.BlockSpec((rows, columns), lambda r: (0, 0)),
        ]
        + unread(before),
        out_specs=pl.BlockSpec((width, columns), lambda r: (r, place)),
        out_shape=jax.ShapeDtypeStruct((left.shape[1], total), BF),
        input_output_aliases={2 + i: i for i in range(len(before))},
        compiler_params=params(),
        cost_estimate=cost(2 * rows * width * count * columns, 4 * rows * columns),
    )(left, right, *before)


def two_terms_kernel(cut, adds, index_ref, left_ref, right_ref, beside_ref, *refs):
    out_ref = refs[-1]
    columns = right_ref.shape[1]
    value = mm(left_ref[...], right_ref[...], 0, 0)
    if adds:
        value = value + refs[0][0, :, :columns].astype(F32)
    out_ref[0, :, :columns] = value.astype(BF)
    high = beside_ref.shape[1]
    wide = beside_ref.shape[2] // cut
    for i in range(cut):
        part = slice(i * high, (i + 1) * high)
        value = beside_ref[0, :, i * wide : (i + 1) * wide]
        if adds:
            value = (value.astype(F32) + refs[0][0, part, columns:].astype(F32)).astype(BF)
        out_ref[0, part, columns:] = value


def two_terms(left, right, width, beside, cut, index, add=None, after=()):
    rows, columns = right.shape
    count = len(index)
    extra = beside.shape[2] // cut
    index = jnp.stack([jnp.asarray(i, jnp.int32) for i in index])
    adds = [] if add is None else [add]
    out = pl.BlockSpec((1, width, columns + extra), lambda r, index: (r, 0, 0))
    return pl.pallas_call(
        functools.partial(two_terms_kernel, cut, len(adds)),
        grid_spec=pltpu.PrefetchScalarGridSpec(
            num_scalar_prefetch=1,
            grid=(count,),
            in_specs=[
                pl.BlockSpec((rows, width), lambda r, index: (0, index[r])),
                pl.BlockSpec((rows, columns), lambda r, index: (0, 0)),
                pl.BlockSpec((1,) + beside.shape[1:], lambda r, index: (index[r], 0, 0)),
            ]
            + [out] * len(adds)
            + unread(after),
            out_specs=out,
        ),
        out_shape=jax.ShapeDtypeStruct((count, width, columns + extra), BF),
        compiler_params=params(),
        cost_estimate=cost(2 * rows * width * count * columns, 4 * rows * columns),
    )(index, left, right, beside, *adds, *after)


def product_kernel(left_ref, right_ref, bias_ref, *refs):
    refs[-1][...] = mm(left_ref[...], right_ref[...]) + bias_ref[...]


def product(left, right, bias, after=()):
    rows, depth = left.shape
    columns = bias.shape[0]
    cut = 512 if columns % 512 == 0 else 256
    return pl.pallas_call(
        product_kernel,
        grid=(columns // cut,),
        in_specs=[
            pl.BlockSpec((rows, depth), lambda j: (0, 0)),
            pl.BlockSpec((depth, cut), lambda j: (0, j)),
            pl.BlockSpec((1, cut), lambda j: (0, j)),
        ]
        + unread(after),
        out_specs=pl.BlockSpec((rows, cut), lambda j: (0, j)),
        out_shape=jax.ShapeDtypeStruct((rows, columns), F32),
        compiler_params=params(),
        cost_estimate=cost(2 * rows * depth * columns, 4 * rows * (depth + columns)),
    )(left, right, bias[None], *after)


def slope_kernel(left_ref, right_ref, slope_ref, *refs):
    value = mm(left_ref[...], right_ref[...], 1, 1) * slope_ref[...].astype(F32)
    refs[-1][...] = value.astype(BF)


def times_slope(left, right, begin, slope, after=()):
    rows, depth = left.shape
    columns = right.shape[0]
    cut = min(512, columns)
    block = pl.BlockSpec((rows, cut), lambda j: (0, j))
    return pl.pallas_call(
        slope_kernel,
        grid=(columns // cut,),
        in_specs=[
            pl.BlockSpec((rows, depth), lambda j: (0, 0)),
            pl.BlockSpec((cut, depth), lambda j: (j, begin // depth)),
            block,
        ]
        + unread(after),
        out_specs=block,
        out_shape=jax.ShapeDtypeStruct(slope.shape, BF),
        compiler_params=params(),
        cost_estimate=cost(2 * rows * depth * columns, 6 * rows * depth),
    )(left, right, slope, *after)


def output_kernel(left_ref, right_ref, second_ref, weight_ref, *refs):
    value = mm(left_ref[...], right_ref[...]) + mm(second_ref[...], weight_ref[...])
    refs[-1][...] = value.astype(BF)


def output_terms(left, right, begin, second, weight, after=()):
    rows, depth = left.shape
    columns = weight.shape[1]
    cut = min(512, columns)
    return pl.pallas_call(
        output_kernel,
        grid=(columns // cut,),
        in_specs=[
            pl.BlockSpec((rows, depth), lambda j: (0, 0)),
            pl.BlockSpec((depth, cut), lambda j: (0, begin // cut + j)),
            pl.BlockSpec(second.shape, lambda j: (0, 0)),
            pl.BlockSpec((second.shape[1], cut), lambda j: (0, j)),
        ]
        + unread(after),
        out_specs=pl.BlockSpec((rows, cut), lambda j: (0, j)),
        out_shape=jax.ShapeDtypeStruct((rows, columns), BF),
        compiler_params=params(),
        cost_estimate=cost(2 * rows * (depth + second.shape[1]) * columns, 6 * rows * depth),
    )(left, right, second, weight, *after)


def normed_kernel(one_ref, first_ref, two_ref, second_ref, in_ref, mean_ref, std_ref, *refs):
    out_ref, gain_ref, shift_ref = refs[-3:]
    value = mm(one_ref[...], first_ref[...], 1, 1) + mm(two_ref[...], second_ref[...], 1, 1)
    out_ref[...] = value.astype(BF)
    normal_hat = (in_ref[...].astype(F32) - mean_ref[...]) * std_ref[...]
    gain_ref[...] = jnp.sum(value * normal_hat, axis=0, keepdims=True)
    shift_ref[...] = jnp.sum(value, axis=0, keepdims=True)


def normed_terms(one, first, two, second, rows_in, mean, std, after=()):
    rows = one.shape[0]
    columns = first.shape[0]
    cut = min(512, columns)
    vector = pl.BlockSpec((1, cut), lambda j: (0, j))

    def whole(array):
        return pl.BlockSpec(array.shape, lambda j: (0, 0))

    return pl.pallas_call(
        normed_kernel,
        grid=(columns // cut,),
        in_specs=[
            whole(one),
            pl.BlockSpec((cut, one.shape[1]), lambda j: (j, 0)),
            whole(two),
            pl.BlockSpec((cut, two.shape[1]), lambda j: (j, 0)),
            pl.BlockSpec((rows, cut), lambda j: (0, j)),
            whole(mean),
            whole(std),
        ]
        + unread(after),
        out_specs=[pl.BlockSpec((rows, cut), lambda j: (0, j)), vector, vector],
        out_shape=[
            jax.ShapeDtypeStruct((rows, columns), BF),
            jax.ShapeDtypeStruct((1, columns), F32),
            jax.ShapeDtypeStruct((1, columns), F32),
        ],
        compiler_params=params(),
        cost_estimate=cost(2 * rows * columns * (one.shape[1] + two.shape[1]), 8 * rows * columns),
    )(one, first, two, second, rows_in, mean, std, *after)


def spread_kernel(width, in_ref, out_ref):
    for s in range(in_ref.shape[0]):
        out_ref[:, s * width : (s + 1) * width] = in_ref[s].astype(F32)


def spread_columns(pieces, width):
    count, rows, columns = pieces.shape
    return pl.pallas_call(
        functools.partial(spread_kernel, width),
        grid=(columns // width,),
        in_specs=[pl.BlockSpec((count, rows, width), lambda i: (0, 0, i))],
        out_specs=pl.BlockSpec((rows, width * count), lambda i: (0, i)),
        out_shape=jax.ShapeDtypeStruct((rows, columns * count), F32),
        compiler_params=params(),
        cost_estimate=cost(0, 6 * rows * columns * count),
    )(pieces)


def heads_kernel(half, in_ref, out_ref):
    parts = []
    for head in range(2):
        for s in range(in_ref.shape[0]):
            for part in range(3):
                start = (2 * part + head) * half
                parts.append(in_ref[s, :, start : start + half].astype(F32))
    for i in range(0, len(parts), 2):
        out_ref[:, i * half : (i + 2) * half] = jnp.concatenate(parts[i : i + 2], axis=1)


def spread_heads(pieces, pairs):
    count, rows, unused = pieces.shape
    width = 6 * HEAD_DIM
    return pl.pallas_call(
        functools.partial(heads_kernel, HEAD_DIM),
        grid=(pairs,),
        in_specs=[pl.BlockSpec((count, rows, width), lambda i: (0, 0, i))],
        out_specs=pl.BlockSpec((rows, width * count), lambda i: (0, i)),
        out_shape=jax.ShapeDtypeStruct((rows, pairs * width * count), F32),
        compiler_params=params(),
        cost_estimate=cost(0, 6 * rows * pairs * width * count),
    )(pieces)


def by_pairs(array, heads):
    lead = array.shape[:-1]
    array = array.reshape(lead + (heads // 2, 2, 3, HEAD_DIM))
    return jnp.swapaxes(array, -3, -2).reshape(lead + (heads * 3 * HEAD_DIM,))


def by_heads(array, heads):
    lead = array.shape[:-1]
    array = array.reshape(lead + (heads // 2, 3, 2, HEAD_DIM))
    return jnp.swapaxes(array, -3, -2).reshape(lead + (heads * 3 * HEAD_DIM,))


def per_device(
    inputs,
    doc_starts,
    ln_gain,
    ln_bias,
    w_qkv,
    b_qkv,
    w_out,
    b_out,
    w_fc1,
    b_fc1,
    w_fc2,
    b_fc2,
    cotangent,
):
    seqs, shards = lax.axis_size("seq"), lax.axis_size("fsdp")
    me = lax.axis_index("seq")
    chips, chip, core = fsdp_place()
    tok, width = inputs.shape[1:]
    length = tok * seqs
    rows_here = w_qkv.shape[0]
    heads = HEADS // seqs
    head_cols = heads * HEAD_DIM
    shard_heads = w_out.shape[0] // HEAD_DIM
    strided = shard_heads % seqs == 0
    each = shard_heads // seqs
    unit = w_fc2.shape[0] // seqs
    hidden_cols = unit * shards
    order = [2 * ((chip + r) % chips) + (core ^ h) for h in (0, 1) for r in range(chips)]

    fc1_here = jnp.concatenate(
        [
            lax.dynamic_slice_in_dim(w_fc1, (i * seqs + me) * unit, unit, 1)
            for i in range(shards)
        ],
        axis=1,
    )
    fc2_here = pick(w_fc2.reshape(seqs, unit, width), me)
    if strided:
        qkv_here = pick(w_qkv.reshape(rows_here, shards, seqs, each * 3 * HEAD_DIM), me, 2)
    else:
        qkv_here = pick(w_qkv.reshape(rows_here, seqs, heads * 3 * HEAD_DIM), me, 1)
    qkv_here = by_pairs(qkv_here.reshape(rows_here, 3 * head_cols), heads)
    out_cut = rows_here // (each * HEAD_DIM) if strided else 1
    if strided:
        out_here = pick(w_out.reshape(seqs, each * HEAD_DIM, width), me)
        out_here = out_here.reshape(each * HEAD_DIM, out_cut, width // out_cut)
        out_here = jnp.swapaxes(out_here, 0, 1).reshape(rows_here, width // out_cut)
        qkv_here = jnp.concatenate([qkv_here, out_here], axis=1)

    sizes = [v.shape[0] for v in (ln_gain, ln_bias, b_out, b_fc2, b_qkv, b_fc1)]
    small = jnp.concatenate([ln_gain, ln_bias, b_out, b_fc2, b_qkv, b_fc1])[None]
    small = lax.all_gather(small, "fsdp", axis=0, tiled=True).astype(F32)
    cuts = [sum(sizes[:i]) for i in range(len(sizes) + 1)]
    gain, shift, bias_out, bias_fc2, bias_qkv, bias_fc1 = [
        small[:, a:b].reshape(-1) for a, b in zip(cuts[:-1], cuts[1:])
    ]
    bias_fc1 = pick(bias_fc1.reshape(shards, seqs, unit), me, 1).reshape(hidden_cols)
    if strided:
        bias_qkv = pick(bias_qkv.reshape(shards, seqs, each * 3 * HEAD_DIM), me, 1)
    else:
        bias_qkv = pick(bias_qkv.reshape(seqs, heads * 3 * HEAD_DIM), me)
    bias_qkv = by_pairs(bias_qkv.reshape(3 * head_cols), heads)

    joined = rows_here == unit and hidden_cols == width and unit % 128 == 0 and shards % 2 == 0
    if joined:
        fc1 = fc2 = fsdp_gather(pick_two(w_fc1, w_fc2, unit))
        begin = hidden_cols
    else:
        fc1, fc2, begin = fsdp_gather(fc1_here), fsdp_gather(fc2_here), 0
    rows_all, grad_rows = seq_gather_two(inputs[0], cotangent[0])
    rows_all, grad_rows = rows_all.reshape(length, width), grad_rows.reshape(length, width)

    starts_row = doc_starts[0]
    pos = jnp.arange(length, dtype=jnp.int32)
    before = starts_row[None, :] <= pos[:, None]
    opening = jnp.max(jnp.where(before, starts_row[None, :], 0), axis=1)
    rates = 10000.0 ** (-2.0 * jnp.arange(ROT // 2, dtype=F32) / ROT)
    angle = (pos - opening).astype(F32)[:, None] * rates[None, :]
    cosine, sine = jnp.cos(angle), jnp.sin(angle)
    rest = jnp.ones((length, HEAD_DIM - ROT), F32)
    cosine = jnp.concatenate([cosine, cosine, rest] * 2, axis=1)
    sine = jnp.concatenate([-sine, sine, 0.0 * rest] * 2, axis=1)

    normed, mean, inv_std = layer_norm(rows_all, behind(gain, grad_rows), shift)
    both = fsdp_gather(behind(qkv_here, normed))
    mine, others = order[:chips], order[chips:]

    active, slope = hidden_layer(normed, fc1, bias_fc1)
    if joined:
        terms = row_terms(active, grad_rows, unit, 2 * width, 0)
        grad_hidden = times_slope(grad_rows, fc2, begin, slope, [terms])
        terms = row_terms(normed, grad_hidden, rows_here, 2 * width, 1, [terms])
        sums = fsdp_sum(terms)
        part_fc2, part_fc1 = sums[:, :width], sums[:, width:]
    else:
        part_fc2 = fsdp_sum(mm(active, grad_rows, 0, 0).astype(BF))
        grad_hidden = times_slope(grad_rows, fc2, begin, slope)
        terms = mm(normed, grad_hidden, 0, 0).astype(BF)
        part_fc1 = fsdp_sum(terms)

    if strided:
        high = each * HEAD_DIM
        out_w, grad_mixed = mixed_gradient(grad_rows, both, 3 * head_cols, out_cut, high, [terms])
    else:
        out_w = pick(fsdp_gather(w_out).reshape(seqs, head_cols, width), me)
        grad_mixed = mm(grad_rows, out_w, 1, 1).astype(BF)
    qkv = product(normed, both, bias_qkv, [grad_mixed])
    tables = (cosine, sine, opening[None])
    mixed, grad_qkv = attention(qkv, grad_mixed, *tables, 0, heads // 2)
    partial = output_terms(active, fc2, begin, mixed, out_w, [grad_qkv])
    result = seq_sum_halves(partial.reshape(seqs, tok, width))
    grad_partial, sum_gain, sum_shift = normed_terms(
        grad_qkv, both, grad_hidden, fc1, rows_all, mean, inv_std, [partial]
    )
    grad_normed = seq_sum_halves(grad_partial.reshape(seqs, tok, width))
    out_grad = mm(mixed, grad_rows, 0, 0).astype(BF)
    if strided:
        out_grad = out_grad.reshape(shards, each * HEAD_DIM, width)
        every = list(range(shards))
        all_qkv = two_terms(
            normed, grad_qkv, rows_here, out_grad, out_cut, every, None, [grad_partial]
        )
        all_qkv = all_qkv.reshape(width, -1)
    else:
        spread = put(jnp.zeros((seqs, head_cols, width), BF), out_grad, me)
        part_out = fsdp_sum(spread.reshape(seqs * head_cols, width))
        all_qkv = mm(normed, grad_qkv, 0, 0).astype(BF)
    part_qkv = fsdp_sum(all_qkv)
    part_fc2 = behind(part_fc2, result)
    if joined:
        whole_fc2, whole_fc1 = seq_gather_two(part_fc2, part_fc1)
    else:
        whole_fc2, whole_fc1 = seq_all(part_fc2), seq_all(part_fc1)
    whole_qkv = seq_all(behind(behind(part_qkv, grad_normed), whole_fc1))
    output = (inputs[0].astype(F32) + result + (bias_out + bias_fc2)).astype(BF)[None]
    sum_gain, sum_shift = sum_gain[0], sum_shift[0]
    own_std = pick(inv_std.reshape(seqs, tok, 1), me)
    own_hat = (inputs[0].astype(F32) - pick(mean.reshape(seqs, tok, 1), me)) * own_std
    scaled = grad_normed * gain
    grad_in = own_std * (
        scaled
        - jnp.mean(scaled, axis=-1, keepdims=True)
        - own_hat * jnp.mean(scaled * own_hat, axis=-1, keepdims=True)
    )
    grad_in = cotangent[0].astype(F32) + grad_in

    sum_bfc1 = jnp.sum(grad_hidden.astype(F32), axis=0).reshape(shards, unit)
    sum_bfc1 = put(jnp.zeros((shards, seqs, unit), F32), sum_bfc1, me, 1)
    sum_bqkv = by_heads(jnp.sum(grad_qkv.astype(F32), axis=0), heads)
    if strided:
        sum_bqkv = sum_bqkv.reshape(shards, each * 3 * HEAD_DIM)
        sum_bqkv = put(jnp.zeros((shards, seqs, each * 3 * HEAD_DIM), F32), sum_bqkv, me, 1)
    else:
        sum_bqkv = put(jnp.zeros((seqs, heads * 3 * HEAD_DIM), F32), sum_bqkv, me)
    sum_out = jnp.sum(cotangent[0].astype(F32), axis=0)
    vectors = jnp.concatenate(
        [v.reshape(shards, -1) for v in (sum_gain, sum_shift, sum_out, sum_bqkv, sum_bfc1)], axis=1
    )
    vectors = vectors[:, None]
    vectors = LineSum(
        jnp.stack([pick(vectors, i) for i in others]),
        lambda got: jnp.stack([pick(vectors, i) for i in mine]) + got,
    ).total
    vectors = jnp.sum(seq_gather(vectors), axis=(0, 1))
    ends = [sizes[0], sizes[1], sizes[2], sizes[4], sizes[5]]
    ends = [sum(ends[:i]) for i in range(len(ends) + 1)]
    total_gain, total_shift, total_bout, total_bqkv, total_bfc1 = [
        vectors[a:b] for a, b in zip(ends[:-1], ends[1:])
    ]

    total_wfc2 = whole_fc2.astype(F32).reshape(seqs * unit, width)
    if unit % 128 == 0:
        total_wfc1 = spread_columns(whole_fc1, unit)
    else:
        total_wfc1 = whole_fc1.astype(F32).reshape(seqs, rows_here, shards, unit)
        total_wfc1 = total_wfc1.transpose(1, 2, 0, 3).reshape(rows_here, -1)
    if strided and each == 1:
        total_wqkv = spread_heads(whole_qkv, heads // 2)
    else:
        total_wqkv = by_heads(whole_qkv[:, :, : 3 * head_cols].astype(F32), heads)
        if strided:
            total_wqkv = total_wqkv.reshape(seqs, rows_here, shards, each * 3 * HEAD_DIM)
            total_wqkv = total_wqkv.transpose(1, 2, 0, 3).reshape(rows_here, -1)
        else:
            total_wqkv = total_wqkv.transpose(1, 0, 2).reshape(rows_here, -1)
    if strided:
        total_wout = whole_qkv[:, :, 3 * head_cols :].astype(F32)
        total_wout = total_wout.reshape(seqs, out_cut, each * HEAD_DIM, width // out_cut)
        total_wout = jnp.swapaxes(total_wout, 1, 2).reshape(-1, width)
    else:
        total_wout = jnp.sum(seq_all(part_out.astype(BF)).astype(F32), axis=0)
    return (
        output,
        grad_in[None],
        total_gain,
        total_shift,
        total_wqkv,
        total_bqkv,
        total_wout,
        total_bout,
        total_wfc1,
        total_bfc1,
        total_wfc2,
        total_bout,
    )


def solution(mesh):
    rows, vector, matrix = P("fsdp", "seq", None), P("fsdp"), P("fsdp", None)
    weights = (vector, vector) + (matrix, vector) * 4
    return jax.shard_map(
        per_device,
        mesh=mesh,
        in_specs=(rows, matrix) + weights + (rows,),
        out_specs=(rows, rows) + weights,
        check_vma=False,
    )
```

```python
import functools

import jax
import jax.numpy as jnp
from jax import lax
from jax.experimental import pallas as pl
from jax.experimental.pallas import tpu as pltpu
from jax.sharding import PartitionSpec as P

HEADS = 32
HEAD_DIM = 64
ROT = 32
EPS = 1e-05
BF = jnp.bfloat16
F32 = jnp.float32
VMEM_BYTES = 56 * 1024 * 1024


def mm(left, right, left_dim=1, right_dim=0):
    return lax.dot_general(
        left, right, (((left_dim,), (right_dim,)), ((), ())), preferred_element_type=F32
    )


def pick(array, index, axis=0):
    return lax.dynamic_index_in_dim(array, index, axis, keepdims=False)


def put(array, piece, index, axis=0):
    return lax.dynamic_update_index_in_dim(array, piece, index, axis)


def behind(array, other):
    first = lax.slice(other, (0,) * other.ndim, (1,) * other.ndim).reshape(())
    return jnp.where(jnp.isnan(first), jnp.zeros((), array.dtype), array)


def unread(arrays):
    return [pl.BlockSpec(memory_space=pl.ANY) for unused in arrays]


def params():
    return pltpu.CompilerParams(vmem_limit_bytes=VMEM_BYTES)


def cost(flops, size, transcendentals=0):
    return pl.CostEstimate(flops=flops, bytes_accessed=size, transcendentals=transcendentals)


def seq_exchange(blocks):
    return lax.all_to_all(blocks, "seq", split_axis=0, concat_axis=0)


def seq_gather(block):
    count = lax.axis_size("seq")
    return seq_exchange(jnp.broadcast_to(block[None], (count,) + block.shape))


def seq_gather_two(first, second):
    me, count = lax.axis_index("seq"), lax.axis_size("seq")
    bits = list(range(count.bit_length() - 1))
    orders = (bits, bits[::-1])
    wholes = [first[None], second[None]]
    late = None
    for step in bits:
        got = []
        for whole, order in zip(wholes, orders):
            pairs = [(i, i ^ (1 << order[step])) for i in range(count)]
            got.append(lax.ppermute(whole, "seq", pairs))
        late = got
        for i, order in enumerate(orders):
            low = (me >> order[step]) % 2 == 0
            whole, new = wholes[i], behind(got[i], got[1 - i])
            whole = jnp.where(low, jnp.stack([whole, new]), jnp.stack([new, whole]))
            wholes[i] = whole.reshape((-1,) + first.shape)
    sizes = (2,) * len(bits) + second.shape
    order = bits[::-1] + [len(bits) + i for i in range(second.ndim)]
    second = wholes[1].reshape(sizes).transpose(order).reshape(wholes[1].shape)
    return wholes[0], second, late


def seq_all(block):
    return lax.all_gather(block, "seq", axis=0)


def seq_sum_halves(blocks):
    me, count = lax.axis_index("seq"), lax.axis_size("seq")
    bits = list(range(count.bit_length() - 1))
    half = blocks.shape[-1] // 2
    orders = (bits, bits[::-1])
    shape = (2,) * len(bits) + blocks.shape[1:-1] + (half,)
    parts = [blocks[..., :half].reshape(shape), blocks[..., half:].reshape(shape)]
    left = [list(bits[::-1]), list(bits[::-1])]
    for step in bits:
        got = []
        for i, order in enumerate(orders):
            mine, axis = (me >> order[step]) % 2, left[i].index(order[step])
            pairs = [(j, j ^ (1 << order[step])) for j in range(count)]
            got.append(lax.ppermute(pick(parts[i], 1 - mine, axis), "seq", pairs))
        for i, order in enumerate(orders):
            mine, axis = (me >> order[step]) % 2, left[i].index(order[step])
            left[i].remove(order[step])
            total = pick(parts[i], mine, axis).astype(F32) + behind(got[i], got[1 - i]).astype(F32)
            parts[i] = total.astype(blocks.dtype) if left[i] else total
    return jnp.concatenate(parts, axis=-1)


def seq_sum(blocks):
    return jnp.sum(seq_exchange(blocks).astype(F32), axis=0)


def fsdp_place():
    me = lax.axis_index("fsdp")
    return lax.axis_size("fsdp") // 2, me // 2, me % 2


def to_chips(array, moves):
    pairs = [(2 * a + core, 2 * b + core) for a, b in moves for core in (0, 1)]
    return lax.ppermute(array, "fsdp", pairs)


def to_other_core(array):
    count = lax.axis_size("fsdp")
    return lax.ppermute(array, "fsdp", [(i, i ^ 1) for i in range(count)])


def fsdp_gather(block):
    return lax.all_gather(block, "fsdp", axis=0, tiled=True)


def fsdp_sum(parts):
    return lax.psum_scatter(parts, "fsdp", scatter_dimension=0, tiled=True)


class LineSum:
    def __init__(self, other, own_of):
        chips, chip, core = fsdp_place()
        own = own_of(to_other_core(other))
        first = jnp.where(chip == 0, own[chips - 1], own[1])
        got = to_chips(first, [(chips - 1, chips - 2), (0, 1)])
        self.first = first
        self.steps = [own, got]
        total = own[0].astype(F32) + got.astype(F32)
        down, up = got, got
        for step in range(2, chips):
            down = (down.astype(F32) + own[step].astype(F32)).astype(own.dtype)
            up = (up.astype(F32) + own[chips - step].astype(F32)).astype(own.dtype)
            down = to_chips(down, [(a, a - 1) for a in range(chips - step, chips)])
            up = to_chips(up, [(a, a + 1) for a in range(0, step)])
            self.steps += [down, up]
        if chips > 2:
            total = own[0].astype(F32) + down.astype(F32) + up.astype(F32)
        self.total = total


def attention_kernel(rows, half, qkv_ref, grad_ref, cos_ref, sin_ref, open_ref, *refs):
    mixed_ref, out_ref, key_ref, value_ref = refs[-4:]
    length = qkv_ref.shape[0]
    wide = 2 * half
    lane = lax.broadcasted_iota(jnp.int32, (length, wide), 1)
    turned = ROT // 2
    leading = (lane % half) < turned
    cosine, sine = cos_ref[...], sin_ref[...]
    scale = half ** (-0.5)

    def turn(x, s):
        other = jnp.where(leading, pltpu.roll(x, wide - turned, 1), pltpu.roll(x, turned, 1))
        return x * cosine + other * s

    query = turn(qkv_ref[:, :wide], sine).astype(BF)
    key = turn(qkv_ref[:, wide : 2 * wide], sine).astype(BF)
    value = qkv_ref[:, 2 * wide :].astype(BF)
    query = (query.astype(F32) * scale).astype(BF)
    grad = grad_ref[...]
    key_t = key.astype(F32).T.astype(BF)
    value_t = value.astype(F32).T.astype(BF)
    key_ref[...] = jnp.zeros_like(key_ref)
    value_ref[...] = jnp.zeros_like(value_ref)
    zero = jnp.zeros((), BF)
    for begin in range(0, length, rows):
        end = begin + rows
        cut = slice(begin, end)
        k_pos = lax.broadcasted_iota(jnp.int32, (end, rows), 0)
        q_pos = lax.broadcasted_iota(jnp.int32, (end, rows), 1) + begin
        allowed = (k_pos <= q_pos) & (k_pos >= open_ref[:, cut])
        side = lane[:rows] < half
        mixed_t, query_t = [], []
        for head in range(2):
            here = side if head == 0 else ~side
            q_rows = jnp.where(here, query[cut], zero)
            g_rows = jnp.where(here, grad[cut], zero)
            scores = jnp.where(allowed, mm(key[:end], q_rows, 1, 1), -1000000000.0)
            expo = jnp.exp(scores - jnp.max(scores, axis=0, keepdims=True))
            probs = expo * (1.0 / jnp.sum(expo, axis=0, keepdims=True))
            low = probs.astype(BF)
            own = slice(head * half, (head + 1) * half)
            mixed_t.append(mm(value_t[own, :end], low))
            grad_probs = mm(value[:end], g_rows, 1, 1)
            dots = jnp.sum(probs * grad_probs, axis=0, keepdims=True)
            grad_scores = (probs * (grad_probs - dots)).astype(BF)
            query_t.append(mm(key_t[own, :end], grad_scores))
            key_ref[:end] += mm(grad_scores, q_rows)
            value_ref[:end] += mm(low, g_rows)
        mixed_ref[cut] = jnp.concatenate(mixed_t, axis=0).T.astype(BF)
        q_grad = jnp.concatenate(query_t, axis=0).T * scale
        lead = leading[:rows]
        other = jnp.where(
            lead, pltpu.roll(q_grad, wide - turned, 1), pltpu.roll(q_grad, turned, 1)
        )
        out_ref[cut, :wide] = (q_grad * cosine[cut] - other * sine[cut]).astype(BF)
    out_ref[:, wide : 2 * wide] = turn(key_ref[...], -sine).astype(BF)
    out_ref[:, 2 * wide :] = value_ref[...].astype(BF)


def attention(qkv, grad, cosine, sine, opening, begin, steps, before=(), after=()):
    length = qkv.shape[0]
    wide = 2 * HEAD_DIM
    pairs = grad.shape[1] // wide

    def whole(array):
        return pl.BlockSpec(array.shape, lambda p: (0, 0))

    narrow = pl.BlockSpec((length, wide), lambda p: (0, begin + p))
    three = pl.BlockSpec((length, 3 * wide), lambda p: (0, begin + p))
    return pl.pallas_call(
        functools.partial(attention_kernel, min(256, length), HEAD_DIM),
        grid=(steps,),
        in_specs=[three, narrow, whole(cosine), whole(sine), whole(opening)]
        + unread(before)
        + unread(after),
        out_specs=[narrow, three],
        out_shape=[
            jax.ShapeDtypeStruct((length, pairs * wide), BF),
            jax.ShapeDtypeStruct((length, pairs * 3 * wide), BF),
        ],
        input_output_aliases={5 + i: i for i in range(len(before))},
        scratch_shapes=[pltpu.VMEM((length, wide), F32), pltpu.VMEM((length, wide), F32)],
        compiler_params=params(),
        cost_estimate=cost(
            24 * length * length * wide * steps,
            24 * length * wide * steps,
            length * length * steps,
        ),
    )(qkv, grad, cosine, sine, opening, *before, *after)


def pick_kernel(me_ref, *refs):
    *pieces, second_ref, out_ref = refs
    step = pl.program_id(0)
    unit = pieces[0].shape[1]

    @pl.when(step < 2)
    def _():
        for i, piece in enumerate(pieces):
            out_ref[:, i * unit : (i + 1) * unit] = piece[...]

    @pl.when(step >= 2)
    def _():
        out_ref[...] = second_ref[...]


def pick_two(first, second, unit):
    seqs = lax.axis_size("seq")
    rows, columns = first.shape[0], first.shape[1] // seqs
    count = columns // unit // 2
    me = lax.axis_index("seq").astype(jnp.int32).reshape(1)

    def piece(i):
        return pl.BlockSpec(
            (rows, unit), lambda j, me: (0, (jnp.minimum(j, 1) * count + i) * seqs + me[0])
        )

    return pl.pallas_call(
        pick_kernel,
        grid_spec=pltpu.PrefetchScalarGridSpec(
            num_scalar_prefetch=1,
            grid=(4,),
            in_specs=[piece(i) for i in range(count)]
            + [
                pl.BlockSpec(
                    (unit, columns // 2), lambda j, me: (me[0], jnp.maximum(j - 2, 0))
                )
            ],
            out_specs=pl.BlockSpec((rows, columns // 2), lambda j, me: (0, j)),
        ),
        out_shape=jax.ShapeDtypeStruct((rows, 2 * columns), BF),
        compiler_params=params(),
        cost_estimate=cost(0, 8 * rows * columns),
    )(me, *([first] * count), second)


def norm_kernel(in_ref, gain_ref, shift_ref, out_ref, mean_ref, std_ref):
    value = in_ref[...].astype(F32)
    mean = jnp.mean(value, axis=-1, keepdims=True)
    centred = value - mean
    std = lax.rsqrt(jnp.mean(centred * centred, axis=-1, keepdims=True) + EPS)
    out_ref[...] = (centred * std * gain_ref[...] + shift_ref[...]).astype(BF)
    mean_ref[...] = mean
    std_ref[...] = std


def layer_norm(rows_in, gain, shift):
    rows, columns = rows_in.shape
    cut = min(256, rows)
    block = pl.BlockSpec((cut, columns), lambda i: (i, 0))
    vector = pl.BlockSpec((1, columns), lambda i: (0, 0))
    narrow = pl.BlockSpec((cut, 1), lambda i: (i, 0))
    return pl.pallas_call(
        norm_kernel,
        grid=(rows // cut,),
        in_specs=[block, vector, vector],
        out_specs=[block, narrow, narrow],
        out_shape=[
            jax.ShapeDtypeStruct((rows, columns), BF),
            jax.ShapeDtypeStruct((rows, 1), F32),
            jax.ShapeDtypeStruct((rows, 1), F32),
        ],
        compiler_params=params(),
        cost_estimate=cost(10 * rows * columns, 4 * rows * columns),
    )(rows_in, gain[None], shift[None])


def mixed_kernel(cut, high, left_ref, both_ref, *refs):
    weight_ref, out_ref = refs[-2:]
    wide = both_ref.shape[1]
    for i in range(both_ref.shape[0] // high):
        rows = slice(i // cut * high, (i // cut + 1) * high)
        columns = slice(i % cut * wide, (i % cut + 1) * wide)
        weight_ref[rows, columns] = both_ref[i * high : (i + 1) * high, :]
    out_ref[...] = mm(left_ref[...], weight_ref[...], 1, 1).astype(BF)


def mixed_gradient(left, both, begin, cut, high, after=()):
    rows, depth = left.shape
    wide = depth // cut
    weight = (both.shape[0] // cut, depth)

    def whole(shape):
        return pl.BlockSpec(shape, lambda i: (0, 0))

    return pl.pallas_call(
        functools.partial(mixed_kernel, cut, high),
        grid=(1,),
        in_specs=[
            whole(left.shape),
            pl.BlockSpec((both.shape[0], wide), lambda i: (0, begin // wide)),
        ]
        + unread(after),
        out_specs=[whole(weight), whole((rows, weight[0]))],
        out_shape=[
            jax.ShapeDtypeStruct(weight, BF),
            jax.ShapeDtypeStruct((rows, weight[0]), BF),
        ],
        compiler_params=params(),
        cost_estimate=cost(2 * rows * depth * weight[0], 4 * rows * depth),
    )(left, both, *after)


def hidden_kernel(left_ref, right_ref, bias_ref, active_ref, slope_ref):
    value = mm(left_ref[...], right_ref[...]) + bias_ref[...]
    square = value * value
    scaled = 0.7978845608028654 * value
    bend = 0.044715 * square
    tanh = jnp.tanh(scaled * (1.0 + bend))
    half = 0.5 * (1.0 + tanh)
    active_ref[...] = (value * half).astype(BF)
    slope = half + 0.5 * (1.0 - tanh * tanh) * scaled * (1.0 + 3.0 * bend)
    slope_ref[...] = slope.astype(BF)


def hidden_layer(left, right, bias):
    rows, depth = left.shape
    columns = bias.shape[0]
    cut = min(512, columns)
    block = pl.BlockSpec((rows, cut), lambda j: (0, j))
    return pl.pallas_call(
        hidden_kernel,
        grid=(columns // cut,),
        in_specs=[
            pl.BlockSpec((rows, depth), lambda j: (0, 0)),
            pl.BlockSpec((depth, cut), lambda j: (0, j)),
            pl.BlockSpec((1, cut), lambda j: (0, j)),
        ],
        out_specs=[block, block],
        out_shape=[jax.ShapeDtypeStruct((rows, columns), BF)] * 2,
        compiler_params=params(),
        cost_estimate=cost(2 * rows * depth * columns, 4 * rows * (depth + columns), rows * columns),
    )(left, right, bias[None])


def term_kernel(adds, index_ref, left_ref, right_ref, *refs):
    value = mm(left_ref[...], right_ref[...], 0, 0)
    if adds:
        value = value + refs[0][0].astype(F32)
    refs[-1][0] = value.astype(BF)


def block_terms(left, right, width, index, add=None, after=()):
    rows, columns = right.shape
    count = len(index)
    if width % 128:
        blocks = [lax.dynamic_slice_in_dim(left, i * width, width, 1) for i in index]
        value = jnp.stack([mm(block, right, 0, 0) for block in blocks])
        return (value if add is None else value + add.astype(F32)).astype(BF)
    index = jnp.stack([jnp.asarray(i, jnp.int32) for i in index])
    adds = [] if add is None else [add]
    out = pl.BlockSpec((1, width, columns), lambda r, index: (r, 0, 0))
    return pl.pallas_call(
        functools.partial(term_kernel, len(adds)),
        grid_spec=pltpu.PrefetchScalarGridSpec(
            num_scalar_prefetch=1,
            grid=(count,),
            in_specs=[
                pl.BlockSpec((rows, width), lambda r, index: (0, index[r])),
                pl.BlockSpec((rows, columns), lambda r, index: (0, 0)),
            ]
            + [out] * len(adds)
            + unread(after),
            out_specs=out,
        ),
        out_shape=jax.ShapeDtypeStruct((count, width, columns), BF),
        compiler_params=params(),
        cost_estimate=cost(2 * rows * width * count * columns, 4 * rows * columns),
    )(index, left, right, *adds, *after)


def rows_kernel(left_ref, right_ref, *refs):
    refs[-1][...] = mm(left_ref[...], right_ref[...], 0, 0).astype(BF)


def row_terms(left, right, width, total, place, before=()):
    rows, columns = right.shape
    count = left.shape[1] // width
    return pl.pallas_call(
        rows_kernel,
        grid=(count,),
        in_specs=[
            pl.BlockSpec((rows, width), lambda r: (0, r)),
            pl.BlockSpec((rows, columns), lambda r: (0, 0)),
        ]
        + unread(before),
        out_specs=pl.BlockSpec((width, columns), lambda r: (r, place)),
        out_shape=jax.ShapeDtypeStruct((left.shape[1], total), BF),
        input_output_aliases={2 + i: i for i in range(len(before))},
        compiler_params=params(),
        cost_estimate=cost(2 * rows * width * count * columns, 4 * rows * columns),
    )(left, right, *before)


def two_terms_kernel(cut, adds, index_ref, left_ref, right_ref, beside_ref, *refs):
    out_ref = refs[-1]
    columns = right_ref.shape[1]
    value = mm(left_ref[...], right_ref[...], 0, 0)
    if adds:
        value = value + refs[0][0, :, :columns].astype(F32)
    out_ref[0, :, :columns] = value.astype(BF)
    high = beside_ref.shape[1]
    wide = beside_ref.shape[2] // cut
    for i in range(cut):
        part = slice(i * high, (i + 1) * high)
        value = beside_ref[0, :, i * wide : (i + 1) * wide]
        if adds:
            value = (value.astype(F32) + refs[0][0, part, columns:].astype(F32)).astype(BF)
        out_ref[0, part, columns:] = value


def two_terms(left, right, width, beside, cut, index, add=None, after=()):
    rows, columns = right.shape
    count = len(index)
    extra = beside.shape[2] // cut
    index = jnp.stack([jnp.asarray(i, jnp.int32) for i in index])
    adds = [] if add is None else [add]
    out = pl.BlockSpec((1, width, columns + extra), lambda r, index: (r, 0, 0))
    return pl.pallas_call(
        functools.partial(two_terms_kernel, cut, len(adds)),
        grid_spec=pltpu.PrefetchScalarGridSpec(
            num_scalar_prefetch=1,
            grid=(count,),
            in_specs=[
                pl.BlockSpec((rows, width), lambda r, index: (0, index[r])),
                pl.BlockSpec((rows, columns), lambda r, index: (0, 0)),
                pl.BlockSpec((1,) + beside.shape[1:], lambda r, index: (index[r], 0, 0)),
            ]
            + [out] * len(adds)
            + unread(after),
            out_specs=out,
        ),
        out_shape=jax.ShapeDtypeStruct((count, width, columns + extra), BF),
        compiler_params=params(),
        cost_estimate=cost(2 * rows * width * count * columns, 4 * rows * columns),
    )(index, left, right, beside, *adds, *after)


def product_kernel(left_ref, right_ref, bias_ref, *refs):
    refs[-1][...] = mm(left_ref[...], right_ref[...]) + bias_ref[...]


def product(left, right, bias, after=()):
    rows, depth = left.shape
    columns = bias.shape[0]
    cut = 512 if columns % 512 == 0 else 256
    return pl.pallas_call(
        product_kernel,
        grid=(columns // cut,),
        in_specs=[
            pl.BlockSpec((rows, depth), lambda j: (0, 0)),
            pl.BlockSpec((depth, cut), lambda j: (0, j)),
            pl.BlockSpec((1, cut), lambda j: (0, j)),
        ]
        + unread(after),
        out_specs=pl.BlockSpec((rows, cut), lambda j: (0, j)),
        out_shape=jax.ShapeDtypeStruct((rows, columns), F32),
        compiler_params=params(),
        cost_estimate=cost(2 * rows * depth * columns, 4 * rows * (depth + columns)),
    )(left, right, bias[None], *after)


def slope_kernel(left_ref, right_ref, slope_ref, *refs):
    value = mm(left_ref[...], right_ref[...], 1, 1) * slope_ref[...].astype(F32)
    refs[-1][...] = value.astype(BF)


def times_slope(left, right, begin, slope, after=()):
    rows, depth = left.shape
    columns = right.shape[0]
    cut = min(512, columns)
    block = pl.BlockSpec((rows, cut), lambda j: (0, j))
    return pl.pallas_call(
        slope_kernel,
        grid=(columns // cut,),
        in_specs=[
            pl.BlockSpec((rows, depth), lambda j: (0, 0)),
            pl.BlockSpec((cut, depth), lambda j: (j, begin // depth)),
            block,
        ]
        + unread(after),
        out_specs=block,
        out_shape=jax.ShapeDtypeStruct(slope.shape, BF),
        compiler_params=params(),
        cost_estimate=cost(2 * rows * depth * columns, 6 * rows * depth),
    )(left, right, slope, *after)


def output_kernel(left_ref, right_ref, second_ref, weight_ref, *refs):
    value = mm(left_ref[...], right_ref[...]) + mm(second_ref[...], weight_ref[...])
    refs[-1][...] = value.astype(BF)


def output_terms(left, right, begin, second, weight, after=()):
    rows, depth = left.shape
    columns = weight.shape[1]
    cut = min(512, columns)
    return pl.pallas_call(
        output_kernel,
        grid=(columns // cut,),
        in_specs=[
            pl.BlockSpec((rows, depth), lambda j: (0, 0)),
            pl.BlockSpec((depth, cut), lambda j: (0, begin // cut + j)),
            pl.BlockSpec(second.shape, lambda j: (0, 0)),
            pl.BlockSpec((second.shape[1], cut), lambda j: (0, j)),
        ]
        + unread(after),
        out_specs=pl.BlockSpec((rows, cut), lambda j: (0, j)),
        out_shape=jax.ShapeDtypeStruct((rows, columns), BF),
        compiler_params=params(),
        cost_estimate=cost(2 * rows * (depth + second.shape[1]) * columns, 6 * rows * depth),
    )(left, right, second, weight, *after)


def normed_kernel(one_ref, first_ref, two_ref, second_ref, in_ref, mean_ref, std_ref, *refs):
    out_ref, gain_ref, shift_ref = refs[-3:]
    value = mm(one_ref[...], first_ref[...], 1, 1) + mm(two_ref[...], second_ref[...], 1, 1)
    out_ref[...] = value.astype(BF)
    normal_hat = (in_ref[...].astype(F32) - mean_ref[...]) * std_ref[...]
    gain_ref[...] = jnp.sum(value * normal_hat, axis=0, keepdims=True)
    shift_ref[...] = jnp.sum(value, axis=0, keepdims=True)


def normed_terms(one, first, two, second, rows_in, mean, std, after=()):
    rows = one.shape[0]
    columns = first.shape[0]
    cut = min(512, columns)
    vector = pl.BlockSpec((1, cut), lambda j: (0, j))

    def whole(array):
        return pl.BlockSpec(array.shape, lambda j: (0, 0))

    return pl.pallas_call(
        normed_kernel,
        grid=(columns // cut,),
        in_specs=[
            whole(one),
            pl.BlockSpec((cut, one.shape[1]), lambda j: (j, 0)),
            whole(two),
            pl.BlockSpec((cut, two.shape[1]), lambda j: (j, 0)),
            pl.BlockSpec((rows, cut), lambda j: (0, j)),
            whole(mean),
            whole(std),
        ]
        + unread(after),
        out_specs=[pl.BlockSpec((rows, cut), lambda j: (0, j)), vector, vector],
        out_shape=[
            jax.ShapeDtypeStruct((rows, columns), BF),
            jax.ShapeDtypeStruct((1, columns), F32),
            jax.ShapeDtypeStruct((1, columns), F32),
        ],
        compiler_params=params(),
        cost_estimate=cost(2 * rows * columns * (one.shape[1] + two.shape[1]), 8 * rows * columns),
    )(one, first, two, second, rows_in, mean, std, *after)


def spread_kernel(width, in_ref, out_ref):
    for s in range(in_ref.shape[0]):
        out_ref[:, s * width : (s + 1) * width] = in_ref[s].astype(F32)


def spread_columns(pieces, width):
    count, rows, columns = pieces.shape
    return pl.pallas_call(
        functools.partial(spread_kernel, width),
        grid=(columns // width,),
        in_specs=[pl.BlockSpec((count, rows, width), lambda i: (0, 0, i))],
        out_specs=pl.BlockSpec((rows, width * count), lambda i: (0, i)),
        out_shape=jax.ShapeDtypeStruct((rows, columns * count), F32),
        compiler_params=params(),
        cost_estimate=cost(0, 6 * rows * columns * count),
    )(pieces)


def heads_kernel(half, in_ref, out_ref):
    parts = []
    for head in range(2):
        for s in range(in_ref.shape[0]):
            for part in range(3):
                start = (2 * part + head) * half
                parts.append(in_ref[s, :, start : start + half].astype(F32))
    for i in range(0, len(parts), 2):
        out_ref[:, i * half : (i + 2) * half] = jnp.concatenate(parts[i : i + 2], axis=1)


def spread_heads(pieces, pairs):
    count, rows, unused = pieces.shape
    width = 6 * HEAD_DIM
    return pl.pallas_call(
        functools.partial(heads_kernel, HEAD_DIM),
        grid=(pairs,),
        in_specs=[pl.BlockSpec((count, rows, width), lambda i: (0, 0, i))],
        out_specs=pl.BlockSpec((rows, width * count), lambda i: (0, i)),
        out_shape=jax.ShapeDtypeStruct((rows, pairs * width * count), F32),
        compiler_params=params(),
        cost_estimate=cost(0, 6 * rows * pairs * width * count),
    )(pieces)


def by_pairs(array, heads):
    lead = array.shape[:-1]
    array = array.reshape(lead + (heads // 2, 2, 3, HEAD_DIM))
    return jnp.swapaxes(array, -3, -2).reshape(lead + (heads * 3 * HEAD_DIM,))


def by_heads(array, heads):
    lead = array.shape[:-1]
    array = array.reshape(lead + (heads // 2, 3, 2, HEAD_DIM))
    return jnp.swapaxes(array, -3, -2).reshape(lead + (heads * 3 * HEAD_DIM,))


def per_device(
    inputs,
    doc_starts,
    ln_gain,
    ln_bias,
    w_qkv,
    b_qkv,
    w_out,
    b_out,
    w_fc1,
    b_fc1,
    w_fc2,
    b_fc2,
    cotangent,
):
    seqs, shards = lax.axis_size("seq"), lax.axis_size("fsdp")
    me = lax.axis_index("seq")
    chips, chip, core = fsdp_place()
    tok, width = inputs.shape[1:]
    length = tok * seqs
    rows_here = w_qkv.shape[0]
    heads = HEADS // seqs
    head_cols = heads * HEAD_DIM
    shard_heads = w_out.shape[0] // HEAD_DIM
    strided = shard_heads % seqs == 0
    each = shard_heads // seqs
    unit = w_fc2.shape[0] // seqs
    hidden_cols = unit * shards
    order = [2 * ((chip + r) % chips) + (core ^ h) for h in (0, 1) for r in range(chips)]

    fc1_here = jnp.concatenate(
        [
            lax.dynamic_slice_in_dim(w_fc1, (i * seqs + me) * unit, unit, 1)
            for i in range(shards)
        ],
        axis=1,
    )
    fc2_here = pick(w_fc2.reshape(seqs, unit, width), me)
    if strided:
        qkv_here = pick(w_qkv.reshape(rows_here, shards, seqs, each * 3 * HEAD_DIM), me, 2)
    else:
        qkv_here = pick(w_qkv.reshape(rows_here, seqs, heads * 3 * HEAD_DIM), me, 1)
    qkv_here = by_pairs(qkv_here.reshape(rows_here, 3 * head_cols), heads)
    out_cut = rows_here // (each * HEAD_DIM) if strided else 1
    if strided:
        out_here = pick(w_out.reshape(seqs, each * HEAD_DIM, width), me)
        out_here = out_here.reshape(each * HEAD_DIM, out_cut, width // out_cut)
        out_here = jnp.swapaxes(out_here, 0, 1).reshape(rows_here, width // out_cut)
        qkv_here = jnp.concatenate([qkv_here, out_here], axis=1)

    sizes = [v.shape[0] for v in (ln_gain, ln_bias, b_out, b_fc2, b_qkv, b_fc1)]
    small = jnp.concatenate([ln_gain, ln_bias, b_out, b_fc2, b_qkv, b_fc1])[None]
    small = lax.all_gather(small, "fsdp", axis=0, tiled=True).astype(F32)
    cuts = [sum(sizes[:i]) for i in range(len(sizes) + 1)]
    gain, shift, bias_out, bias_fc2, bias_qkv, bias_fc1 = [
        small[:, a:b].reshape(-1) for a, b in zip(cuts[:-1], cuts[1:])
    ]
    bias_fc1 = pick(bias_fc1.reshape(shards, seqs, unit), me, 1).reshape(hidden_cols)
    if strided:
        bias_qkv = pick(bias_qkv.reshape(shards, seqs, each * 3 * HEAD_DIM), me, 1)
    else:
        bias_qkv = pick(bias_qkv.reshape(seqs, heads * 3 * HEAD_DIM), me)
    bias_qkv = by_pairs(bias_qkv.reshape(3 * head_cols), heads)

    joined = rows_here == unit and hidden_cols == width and unit % 128 == 0 and shards % 2 == 0
    if joined:
        fc1 = fc2 = fsdp_gather(pick_two(w_fc1, w_fc2, unit))
        begin = hidden_cols
    else:
        fc1, fc2, begin = fsdp_gather(fc1_here), fsdp_gather(fc2_here), 0
    rows_all, grad_rows, unused = seq_gather_two(inputs[0], cotangent[0])
    rows_all, grad_rows = rows_all.reshape(length, width), grad_rows.reshape(length, width)

    starts_row = doc_starts[0]
    pos = jnp.arange(length, dtype=jnp.int32)
    before = starts_row[None, :] <= pos[:, None]
    opening = jnp.max(jnp.where(before, starts_row[None, :], 0), axis=1)
    rates = 10000.0 ** (-2.0 * jnp.arange(ROT // 2, dtype=F32) / ROT)
    angle = (pos - opening).astype(F32)[:, None] * rates[None, :]
    cosine, sine = jnp.cos(angle), jnp.sin(angle)
    rest = jnp.ones((length, HEAD_DIM - ROT), F32)
    cosine = jnp.concatenate([cosine, cosine, rest] * 2, axis=1)
    sine = jnp.concatenate([-sine, sine, 0.0 * rest] * 2, axis=1)

    normed, mean, inv_std = layer_norm(rows_all, behind(gain, grad_rows), shift)
    both = fsdp_gather(behind(qkv_here, normed))
    mine, others = order[:chips], order[chips:]

    active, slope = hidden_layer(normed, fc1, bias_fc1)
    if joined:
        terms = row_terms(active, grad_rows, unit, 2 * width, 0)
        grad_hidden = times_slope(grad_rows, fc2, begin, slope, [terms])
        terms = row_terms(normed, grad_hidden, rows_here, 2 * width, 1, [terms])
        sums = fsdp_sum(terms)
        part_fc2, part_fc1 = sums[:, :width], sums[:, width:]
    else:
        part_fc2 = fsdp_sum(mm(active, grad_rows, 0, 0).astype(BF))
        grad_hidden = times_slope(grad_rows, fc2, begin, slope)
        terms = mm(normed, grad_hidden, 0, 0).astype(BF)
        part_fc1 = fsdp_sum(terms)

    if strided:
        high = each * HEAD_DIM
        out_w, grad_mixed = mixed_gradient(grad_rows, both, 3 * head_cols, out_cut, high, [terms])
    else:
        out_w = pick(fsdp_gather(w_out).reshape(seqs, head_cols, width), me)
        grad_mixed = mm(grad_rows, out_w, 1, 1).astype(BF)
    qkv = product(normed, both, bias_qkv, [grad_mixed])
    tables = (cosine, sine, opening[None])
    mixed, grad_qkv = attention(qkv, grad_mixed, *tables, 0, heads // 2)
    partial = output_terms(active, fc2, begin, mixed, out_w, [grad_qkv])
    result = seq_sum_halves(partial.reshape(seqs, tok, width))
    grad_partial, sum_gain, sum_shift = normed_terms(
        grad_qkv, both, grad_hidden, fc1, rows_all, mean, inv_std, [partial]
    )
    grad_normed = seq_sum_halves(grad_partial.reshape(seqs, tok, width))
    out_grad = mm(mixed, grad_rows, 0, 0).astype(BF)
    if strided:
        out_grad = out_grad.reshape(shards, each * HEAD_DIM, width)
        every = list(range(shards))
        all_qkv = two_terms(
            normed, grad_qkv, rows_here, out_grad, out_cut, every, None, [grad_partial]
        )
        all_qkv = all_qkv.reshape(width, -1)
    else:
        spread = put(jnp.zeros((seqs, head_cols, width), BF), out_grad, me)
        part_out = fsdp_sum(spread.reshape(seqs * head_cols, width))
        all_qkv = mm(normed, grad_qkv, 0, 0).astype(BF)
    part_qkv = fsdp_sum(all_qkv)
    part_fc2 = behind(part_fc2, result)
    if joined:
        whole_fc2, whole_fc1, brought = seq_gather_two(part_fc2, part_fc1)
    else:
        whole_fc2, whole_fc1 = seq_all(part_fc2), seq_all(part_fc1)
        brought = [whole_fc1, whole_fc2]
    part_qkv = behind(behind(part_qkv, brought[0]), brought[1])
    whole_qkv = seq_all(behind(part_qkv, grad_normed))
    output = (inputs[0].astype(F32) + result + (bias_out + bias_fc2)).astype(BF)[None]
    sum_gain, sum_shift = sum_gain[0], sum_shift[0]
    own_std = pick(inv_std.reshape(seqs, tok, 1), me)
    own_hat = (inputs[0].astype(F32) - pick(mean.reshape(seqs, tok, 1), me)) * own_std
    scaled = grad_normed * gain
    grad_in = own_std * (
        scaled
        - jnp.mean(scaled, axis=-1, keepdims=True)
        - own_hat * jnp.mean(scaled * own_hat, axis=-1, keepdims=True)
    )
    grad_in = cotangent[0].astype(F32) + grad_in

    sum_bfc1 = jnp.sum(grad_hidden.astype(F32), axis=0).reshape(shards, unit)
    sum_bfc1 = put(jnp.zeros((shards, seqs, unit), F32), sum_bfc1, me, 1)
    sum_bqkv = by_heads(jnp.sum(grad_qkv.astype(F32), axis=0), heads)
    if strided:
        sum_bqkv = sum_bqkv.reshape(shards, each * 3 * HEAD_DIM)
        sum_bqkv = put(jnp.zeros((shards, seqs, each * 3 * HEAD_DIM), F32), sum_bqkv, me, 1)
    else:
        sum_bqkv = put(jnp.zeros((seqs, heads * 3 * HEAD_DIM), F32), sum_bqkv, me)
    sum_out = jnp.sum(cotangent[0].astype(F32), axis=0)
    vectors = jnp.concatenate(
        [v.reshape(shards, -1) for v in (sum_gain, sum_shift, sum_out, sum_bqkv, sum_bfc1)], axis=1
    )
    vectors = vectors[:, None]
    vectors = LineSum(
        jnp.stack([pick(vectors, i) for i in others]),
        lambda got: jnp.stack([pick(vectors, i) for i in mine]) + got,
    ).total
    vectors = jnp.sum(seq_gather(vectors), axis=(0, 1))
    ends = [sizes[0], sizes[1], sizes[2], sizes[4], sizes[5]]
    ends = [sum(ends[:i]) for i in range(len(ends) + 1)]
    total_gain, total_shift, total_bout, total_bqkv, total_bfc1 = [
        vectors[a:b] for a, b in zip(ends[:-1], ends[1:])
    ]

    total_wfc2 = whole_fc2.astype(F32).reshape(seqs * unit, width)
    if unit % 128 == 0:
        total_wfc1 = spread_columns(whole_fc1, unit)
    else:
        total_wfc1 = whole_fc1.astype(F32).reshape(seqs, rows_here, shards, unit)
        total_wfc1 = total_wfc1.transpose(1, 2, 0, 3).reshape(rows_here, -1)
    if strided and each == 1:
        total_wqkv = spread_heads(whole_qkv, heads // 2)
    else:
        total_wqkv = by_heads(whole_qkv[:, :, : 3 * head_cols].astype(F32), heads)
        if strided:
            total_wqkv = total_wqkv.reshape(seqs, rows_here, shards, each * 3 * HEAD_DIM)
            total_wqkv = total_wqkv.transpose(1, 2, 0, 3).reshape(rows_here, -1)
        else:
            total_wqkv = total_wqkv.transpose(1, 0, 2).reshape(rows_here, -1)
    if strided:
        total_wout = whole_qkv[:, :, 3 * head_cols :].astype(F32)
        total_wout = total_wout.reshape(seqs, out_cut, each * HEAD_DIM, width // out_cut)
        total_wout = jnp.swapaxes(total_wout, 1, 2).reshape(-1, width)
    else:
        total_wout = jnp.sum(seq_all(part_out.astype(BF)).astype(F32), axis=0)
    return (
        output,
        grad_in[None],
        total_gain,
        total_shift,
        total_wqkv,
        total_bqkv,
        total_wout,
        total_bout,
        total_wfc1,
        total_bfc1,
        total_wfc2,
        total_bout,
    )


def solution(mesh):
    rows, vector, matrix = P("fsdp", "seq", None), P("fsdp"), P("fsdp", None)
    weights = (vector, vector) + (matrix, vector) * 4
    return jax.shard_map(
        per_device,
        mesh=mesh,
        in_specs=(rows, matrix) + weights + (rows,),
        out_specs=(rows, rows) + weights,
        check_vma=False,
    )
```
